256 devices in a mesh: dp: 16 (over z_hi, x, core), tensor: 16 (over y, z_lo).
Axes of the slice: x: 4, y: 4, z: 8 (z_hi: 2, z_lo: 4; z = z_hi * 4 + z_lo), core: 2. Of those that a mesh axis runs over, the one named last changes fastest.
Arguments:
- gate_inputs: bfloat16 [4096, 30720], P('dp', 'tensor'), parts along dimension 0, may hold values from -6 to 6
- up_inputs: bfloat16 [4096, 30720], P('dp', 'tensor'), parts along dimension 0, may hold values from -6 to 6
- down_codes: float32 [5120, 8192], P('tensor'), may hold values from -8388608 to 8388607, as said below
- column_scale: float32 [8192], replicated, may hold values from 0.0008 to 0.004
Outputs:
- mixed: bfloat16 [4096, 8192], P(('dp', 'tensor')), parts along dimension 0
The draws below stay inside these ranges and needn't reach their ends.
There are 16 independent parts, one for each index of `dp`. The reference program is written for one: setup_inputs(seed, part) draws one part's arguments, and reference() takes and returns one part's arrays. A program takes and returns all parts, laid end to end along the dimension named above; an argument that names none is the same for every part. Nothing has to cross between parts.
Inputs may be any that keep to these rules, and one draw needn't show every extreme that they name: `down_codes`: every entry is a whole number; the six base-16 digits of the entry plus 8388608 are independent 4-bit levels of six consecutive hidden units.
All inputs are finite; a program needn't handle non-finite values.
Results may differ from the reference program's by a relative error of at most 0.027.
Values may be sent and summed in bfloat16 or wider, within the bound.
A program may use at most 128 MiB of HBM per device.

```python
import math
import jax
import jax.numpy as jnp
from jax import lax

D = 8192
FF = 30720
ROWS = 256
N_TENSOR = 16


def draw_down_codes(key, part):
    key = jax.random.fold_in(key, 7)
    packed = jnp.zeros((FF // 6, D), jnp.int32)
    for position in range(6):
        digit_draw = jax.random.randint(jax.random.fold_in(key, position), (FF // 6, D), 0, 16, dtype=jnp.int32)
        packed = packed * 16 + digit_draw
    return (packed - 8388608).astype(jnp.float32)


def level_of(own_key, dims, cuts, least, largest):
    def one(dim, parts):
        steps = jax.random.uniform(jax.random.fold_in(jax.random.fold_in(own_key, 6), dim), (parts,), jnp.float32, least / len(cuts), largest / len(cuts))
        return jnp.repeat(jnp.exp(steps), dims[dim] // parts).reshape((-1,) + (1,) * (len(dims) - dim - 1))

    level = one(*cuts[0])
    for cut in cuts[1:]:
        level = level * one(*cut)
    return level


def bell_draw(key, shape, spread, bound, cuts=(), kind=jnp.bfloat16):
    factor_of = level_of(key, shape, cuts, -0.22, 0.18) if cuts else 1.0
    array = jax.random.normal(key, shape, jnp.float32) * spread * factor_of
    return jnp.minimum(jnp.maximum(array, -bound), bound).astype(kind)


def setup_inputs(seed: int = 0, part: int = 0) -> dict:
    streams_of = jax.random.split(jax.random.key(seed), 5)
    own_keys = jax.random.split(jax.random.fold_in(streams_of[4], part), 5)
    gate_inputs = bell_draw(own_keys[0], (ROWS, FF), 1.0, 6.0, ((1, 16),))
    up_inputs = bell_draw(own_keys[1], (ROWS, FF), 1.0, 6.0, ((1, 16),))
    down_codes = draw_down_codes(jax.random.fold_in(streams_of[4], 71), part)
    column_scale = jnp.clip(jnp.exp(jax.random.uniform(streams_of[3], (D,), jnp.float32, math.log(0.0008), math.log(0.004))), 0.0008, 0.004)
    return dict(gate_inputs=gate_inputs, up_inputs=up_inputs, down_codes=down_codes, column_scale=column_scale)


def sylvester(extent):
    indices = jnp.arange(extent, dtype=jnp.int32)
    common = jnp.bitwise_and(indices[:, None], indices[None, :])
    parity = jnp.zeros((extent, extent), jnp.int32)
    for offset in range(extent.bit_length() - 1):
        parity = parity + jnp.bitwise_and(jnp.right_shift(common, offset), 1)
    return (1 - 2 * (parity % 2)).astype(jnp.float32)

def decode_levels(code_block):
    shifted = code_block + 8388608.0
    digit_list = []
    for position in range(6):
        digit_value = jnp.mod(jnp.floor(shifted / 16.0 ** position), 16.0)
        digit_list.append(digit_value)
    stacked = jnp.stack(digit_list, axis=1)
    stacked = stacked.reshape(code_block.shape[0] * 6, code_block.shape[1])
    return (stacked - 8.0).astype(jnp.bfloat16)

def reference(gate_inputs, up_inputs, down_codes, column_scale):
    hidden = (jax.nn.silu(gate_inputs.astype(jnp.float32)) * up_inputs.astype(jnp.float32)).astype(jnp.bfloat16)
    row_total = hidden.shape[0]
    shards = N_TENSOR
    hidden_width = FF // shards
    groups = hidden_width // 128
    blocks = hidden.astype(jnp.float32).reshape(row_total, shards, groups, 128)
    crossed = jnp.einsum('st,rtgj->rsgj', sylvester(shards), blocks, precision=lax.Precision.HIGHEST)
    local_turn = jnp.einsum('rsgj,kj->rsgk', crossed, sylvester(128), precision=lax.Precision.HIGHEST)
    scaling = 1.0 / math.sqrt(128 * shards)
    rotated = (local_turn * scaling).astype(jnp.bfloat16).reshape(row_total, FF)
    shard_rot = rotated.reshape(row_total, shards, hidden_width).transpose(1, 0, 2)
    shard_codes = down_codes.reshape(shards, hidden_width // 6, D)

    def one_shard(carry, shard_pair):
        rot_piece, code_piece = shard_pair
        levels = decode_levels(code_piece)
        shard_term = jnp.dot(rot_piece, levels, preferred_element_type=jnp.float32) * column_scale
        return (carry + shard_term.astype(jnp.bfloat16).astype(jnp.float32), None)
    total, unused = lax.scan(one_shard, jnp.zeros((row_total, D), jnp.float32), (shard_rot, shard_codes))
    return total.astype(jnp.bfloat16)
```

```python
import functools
import math

import jax
import jax.numpy as jnp
import ml_dtypes
import numpy as np
from jax import lax
from jax.experimental import pallas as pl
from jax.experimental.pallas import tpu as pltpu
from jax.sharding import PartitionSpec as P

MESH = pl.DeviceIdType.MESH
NY, NZ, RUN = 4, 8, 4
SHARDS = NY * RUN
SUPER = 384
CODE_ROWS = SUPER // 6
LAG_B, LAG_C, LAG_D = 2, 4, 6


def sylvester(extent):
    indices = np.arange(extent)
    common = indices[:, None] & indices[None, :]
    parity = np.zeros((extent, extent), np.int64)
    for offset in range(extent.bit_length() - 1):
        parity += (common >> offset) & 1
    return 1 - 2 * (parity % 2)


def turn_matrix():
    blocks = np.kron(np.eye(SUPER // 128), sylvester(128))
    order = np.arange(SUPER).reshape(CODE_ROWS, 6).T.reshape(-1)
    return blocks[:, order].astype(ml_dtypes.bfloat16)


def kernel(
    half,
    width,
    gate_hbm,
    up_hbm,
    codes_hbm,
    scale_ref,
    turn_ref,
    out_ref,
    gate,
    up,
    codes,
    hidden,
    gathered,
    turned,
    rot,
    levels,
    part,
    from_below_a,
    from_above_a,
    from_below_b,
    from_above_b,
    from_z,
    load_sem,
    code_sem,
    gather_send,
    gather_recv,
    scatter_send,
    scatter_recv,
    a_send,
    a_recv,
    b_send,
    b_recv,
    z_send,
    z_recv,
):
    rows, hidden_width = gate.shape
    features = levels.shape[1]
    supers = hidden_width // SUPER
    piece = rows // SHARDS
    block = rows // NY
    chunks = features // width
    dp = lax.axis_index("dp")
    me = lax.axis_index("tensor")
    rest = lax.rem(dp, half)
    y = lax.div(me, RUN)
    z_lo = lax.rem(me, RUN)
    z = lax.div(dp, half) * RUN + z_lo
    z_far = lax.rem(z + 6 - 4 * lax.div(z_lo, 2), NZ)
    z_of = (z, lax.rem(z + 1, NZ), lax.rem(z + NZ - 1, NZ), z_far)
    slot_there = (0, 2, 1, 3)

    def device(y_there, z_there):
        return (lax.div(z_there, RUN) * half + rest, y_there * RUN + lax.rem(z_there, RUN))

    def y_of(apart):
        return lax.rem(y + apart, NY)

    def wait_for(ref, sem):
        pltpu.make_async_copy(ref, ref, sem).wait()

    def send(src, dst, send_sem, recv_sem, where):
        pltpu.make_async_remote_copy(
            src_ref=src, dst_ref=dst, send_sem=send_sem, recv_sem=recv_sem, device_id=where, device_id_type=MESH
        ).start()

    barrier = pltpu.get_barrier_semaphore()

    def greet(apart, carry):
        pl.semaphore_signal(barrier, inc=1, device_id=(dp, lax.rem(me + apart, SHARDS)), device_id_type=MESH)
        return carry

    load_gate = pltpu.make_async_copy(gate_hbm, gate, load_sem.at[0])
    load_up = pltpu.make_async_copy(up_hbm, up, load_sem.at[1])
    load_gate.start()
    load_up.start()
    lax.fori_loop(1, SHARDS, greet, 0)
    for slot in (1, 2, 3):

        @pl.when(lax.div(z_of[slot], RUN) != lax.div(z, RUN))
        def _(slot=slot):
            def greet_across(apart, carry):
                pl.semaphore_signal(
                    barrier, inc=1, device_id=device(y_of(apart), z_of[slot]), device_id_type=MESH
                )
                return carry

            lax.fori_loop(0, NY, greet_across, 0)

    def code_copy(q):
        span = pl.ds(pl.multiple_of(q * CODE_ROWS, CODE_ROWS), CODE_ROWS)
        return pltpu.make_async_copy(codes_hbm.at[span, :], codes.at[span, :], code_sem.at[q])

    for q in range(supers):
        code_copy(q).start()
    load_gate.wait()
    load_up.wait()
    across = 1 + lax.rem(lax.div(z_lo + 1, 2) + 1, 2)
    pl.semaphore_wait(barrier, SHARDS - 1 + NY * across)

    def send_hidden(q, carry):
        span = pl.ds(pl.multiple_of(q * SUPER, 128), SUPER)

        def hidden_of(owner):
            its = pl.ds(pl.multiple_of(owner * piece, piece), piece)
            g = gate[its, span].astype(jnp.float32)
            value = g / (1.0 + jnp.exp(-g)) * up[its, span].astype(jnp.float32)
            return its, value.astype(jnp.bfloat16)

        mine = pl.ds(pl.multiple_of(me * piece, piece), piece)
        for apart in range(1, SHARDS):
            owner = lax.rem(me + apart, SHARDS)
            its, value = hidden_of(owner)
            hidden[its, span] = value
            send(
                hidden.at[its, span], gathered.at[mine, span], gather_send, gather_recv.at[q], (dp, owner)
            )
        its, value = hidden_of(me)
        gathered[its, span] = value
        return carry

    lax.fori_loop(0, supers, send_hidden, 0)

    def rotate(q, carry):
        span = pl.ds(pl.multiple_of(q * SUPER, 128), SUPER)
        code_copy(q).wait()

        def decode(tile, inner):
            columns = pl.ds(pl.multiple_of(tile * 256, 256), 256)
            code_span = pl.ds(pl.multiple_of(q * CODE_ROWS, CODE_ROWS), CODE_ROWS)
            shifted = codes[code_span, columns].astype(jnp.int32) + 8388608
            for digit in range(6):
                value = jnp.bitwise_and(jnp.right_shift(shifted, 4 * digit), 15) - 8
                level_span = pl.ds(pl.multiple_of(q * SUPER + digit * CODE_ROWS, CODE_ROWS), CODE_ROWS)
                levels[level_span, columns] = value.astype(jnp.float32).astype(jnp.bfloat16)
            return inner

        lax.fori_loop(0, features // 256, decode, 0)
        wait_for(gathered.at[pl.ds(0, (SHARDS - 1) * piece), span], gather_recv.at[q])
        local = jnp.dot(gathered[:, span], turn_ref[...], preferred_element_type=jnp.float32)
        terms = [local[piece * t : piece * (t + 1)] for t in range(SHARDS)]
        step = 1
        while step < SHARDS:
            after = list(terms)
            for t in range(SHARDS):
                if not t & step:
                    after[t] = terms[t] + terms[t + step]
                    after[t + step] = terms[t] - terms[t + step]
            terms, step = after, 2 * step
        scaling = 1.0 / math.sqrt(128 * SHARDS)
        for t in range(SHARDS):
            turned[piece * t : piece * (t + 1), span] = (terms[t] * scaling).astype(jnp.bfloat16)
        for slot in (3, 1, 2, 0):
            for apart in (2, 1, 3, 0):
                if slot == 0 and apart == 0:
                    continue
                shard = y_of(apart) * RUN + lax.rem(z_of[slot], RUN)
                row = (((NY - apart) % NY) * 4 + slot_there[slot]) * piece
                send(
                    turned.at[pl.ds(pl.multiple_of(shard * piece, piece), piece), span],
                    rot.at[pl.ds(row, piece), span],
                    scatter_send,
                    scatter_recv.at[q],
                    device(y_of(apart), z_of[slot]),
                )
        rot[0:piece, span] = turned[pl.ds(pl.multiple_of(me * piece, piece), piece), span]
        return carry

    lax.fori_loop(0, supers, rotate, 0)

    def wait_rotated(q, carry):
        span = pl.ds(pl.multiple_of(q * SUPER, 128), SUPER)
        wait_for(rot.at[pl.ds(0, (SHARDS - 1) * piece), span], scatter_recv.at[q])
        return carry

    lax.fori_loop(0, supers, wait_rotated, 0)

    def columns_of(c):
        return pl.ds(pl.multiple_of(c * width, width), width)

    def half_of(c):
        return pl.ds(pl.multiple_of(c * (width // 2), width // 2), width // 2)

    def lower_of(c):
        return pl.ds(pl.multiple_of(c * width, width // 2), width // 2)

    def upper_of(c):
        return pl.ds(pl.multiple_of(c * width + width // 2, width // 2), width // 2)

    def added(*values):
        total = values[0].astype(jnp.float32)
        for value in values[1:]:
            total = total + value.astype(jnp.float32)
        return total.astype(jnp.bfloat16)

    above, below = device(y_of(1), z), device(y_of(NY - 1), z)
    own, next_y, opposite, last_y = (pl.ds(block * i, block) for i in range(NY))

    def step(t, carry):
        @pl.when(t < chunks)
        def _():
            c = t
            product = jnp.dot(rot[...], levels[:, columns_of(c)], preferred_element_type=jnp.float32)
            part[:, columns_of(c)] = (product * scale_ref[:, columns_of(c)]).astype(jnp.bfloat16)
            send(part.at[opposite, lower_of(c)], from_below_a.at[:, half_of(c)], a_send, a_recv.at[0, c], above)
            send(part.at[opposite, upper_of(c)], from_above_a.at[:, half_of(c)], a_send, a_recv.at[1, c], below)

        @pl.when((t >= LAG_B) & (t < chunks + LAG_B))
        def _():
            c = t - LAG_B
            wait_for(from_below_a.at[:, half_of(c)], a_recv.at[0, c])
            part[next_y, lower_of(c)] = added(part[next_y, lower_of(c)], from_below_a[:, half_of(c)])
            send(part.at[next_y, columns_of(c)], from_below_b.at[:, columns_of(c)], b_send, b_recv.at[0, c], above)
            wait_for(from_above_a.at[:, half_of(c)], a_recv.at[1, c])
            part[last_y, upper_of(c)] = added(part[last_y, upper_of(c)], from_above_a[:, half_of(c)])
            send(part.at[last_y, columns_of(c)], from_above_b.at[:, columns_of(c)], b_send, b_recv.at[1, c], below)

        @pl.when((t >= LAG_C) & (t < chunks + LAG_C))
        def _():
            c = t - LAG_C
            wait_for(from_below_b.at[:, columns_of(c)], b_recv.at[0, c])
            wait_for(from_above_b.at[:, columns_of(c)], b_recv.at[1, c])
            part[own, columns_of(c)] = added(
                part[own, columns_of(c)], from_below_b[:, columns_of(c)], from_above_b[:, columns_of(c)]
            )
            for slot in (3, 1, 2):
                send(
                    part.at[pl.ds(slot * piece, piece), columns_of(c)],
                    from_z.at[pl.ds((slot_there[slot] - 1) * piece, piece), columns_of(c)],
                    z_send,
                    z_recv.at[slot_there[slot] - 1, c],
                    device(y, z_of[slot]),
                )

        @pl.when(t >= LAG_D)
        def _():
            c = t - LAG_D
            for slot in range(3):
                wait_for(from_z.at[pl.ds(slot * piece, piece), columns_of(c)], z_recv.at[slot, c])
            out_ref[:, columns_of(c)] = added(
                part[pl.ds(0, piece), columns_of(c)],
                *(from_z[pl.ds(slot * piece, piece), columns_of(c)] for slot in range(3)),
            )

        return carry

    lax.fori_loop(0, chunks + LAG_D, step, 0)

    wait_for(gathered.at[pl.ds(0, (SHARDS - 1) * piece), :], gather_send)
    wait_for(rot.at[pl.ds(0, (SHARDS - 1) * piece), :], scatter_send)
    wait_for(part.at[opposite, :], a_send)
    wait_for(part.at[pl.ds(0, 2 * block), :], b_send)
    wait_for(from_z, z_send)


def body(gate_inputs, up_inputs, down_codes, column_scale, half):
    rows, hidden_width = gate_inputs.shape
    code_rows, features = down_codes.shape
    width = min(512, features // 2)
    chunks = features // width
    supers = hidden_width // SUPER
    piece, block = rows // SHARDS, rows // NY
    whole = pl.BlockSpec(memory_space=pltpu.VMEM)
    outside = pl.BlockSpec(memory_space=pl.ANY)
    b16 = jnp.bfloat16
    return pl.pallas_call(
        functools.partial(kernel, half, width),
        out_shape=jax.ShapeDtypeStruct((piece, features), b16),
        in_specs=[outside, outside, outside, whole, whole],
        out_specs=whole,
        scratch_shapes=[
            pltpu.VMEM((rows, hidden_width), b16),
            pltpu.VMEM((rows, hidden_width), b16),
            pltpu.VMEM((code_rows, features), jnp.float32),
            pltpu.VMEM((rows, hidden_width), b16),
            pltpu.VMEM((rows, hidden_width), b16),
            pltpu.VMEM((rows, hidden_width), b16),
            pltpu.VMEM((rows, hidden_width), b16),
            pltpu.VMEM((hidden_width, features), b16),
            pltpu.VMEM((rows, features), b16),
            pltpu.VMEM((block, features // 2), b16),
            pltpu.VMEM((block, features // 2), b16),
            pltpu.VMEM((block, features), b16),
            pltpu.VMEM((block, features), b16),
            pltpu.VMEM((3 * piece, features), b16),
            pltpu.SemaphoreType.DMA((2,)),
            pltpu.SemaphoreType.DMA((supers,)),
            pltpu.SemaphoreType.DMA,
            pltpu.SemaphoreType.DMA((supers,)),
            pltpu.SemaphoreType.DMA,
            pltpu.SemaphoreType.DMA((supers,)),
            pltpu.SemaphoreType.DMA,
            pltpu.SemaphoreType.DMA((2, chunks)),
            pltpu.SemaphoreType.DMA,
            pltpu.SemaphoreType.DMA((2, chunks)),
            pltpu.SemaphoreType.DMA,
            pltpu.SemaphoreType.DMA((3, chunks)),
        ],
        compiler_params=pltpu.CompilerParams(
            collective_id=0, has_side_effects=True, vmem_limit_bytes=60 * 1024 * 1024
        ),
    )(gate_inputs, up_inputs, down_codes, column_scale.reshape(1, features), jnp.asarray(turn_matrix()))


def solution(mesh):
    return jax.shard_map(
        functools.partial(body, half=mesh.shape["dp"] // 2),
        mesh=mesh,
        in_specs=(P("dp", "tensor"), P("dp", "tensor"), P("tensor", None), P()),
        out_specs=P(("dp", "tensor"), None),
        check_vma=False,
    )
```

```python
import functools
import math

import jax
import jax.numpy as jnp
import ml_dtypes
import numpy as np
from jax import lax
from jax.experimental import pallas as pl
from jax.experimental.pallas import tpu as pltpu
from jax.sharding import PartitionSpec as P

MESH = pl.DeviceIdType.MESH
NY, NZ, RUN = 4, 8, 4
SHARDS = NY * RUN
SUPER = 384
CODE_ROWS = SUPER // 6
PATTERN = ((384, 128), (384, 128), (384, 128), (256, 256))
PERIOD = len(PATTERN)
WIDTH = sum(PATTERN[0])
FIRST = 2
Z_SPAN = sum(z_width for _, z_width in PATTERN)
LAG_B, LAG_C, LAG_D = 6, 10, 14


def sylvester(extent):
    indices = np.arange(extent)
    common = indices[:, None] & indices[None, :]
    parity = np.zeros((extent, extent), np.int64)
    for offset in range(extent.bit_length() - 1):
        parity += (common >> offset) & 1
    return 1 - 2 * (parity % 2)


def turn_matrix():
    blocks = np.kron(np.eye(SUPER // 128), sylvester(128))
    order = np.arange(SUPER).reshape(CODE_ROWS, 6).T.reshape(-1)
    return blocks[:, order].astype(ml_dtypes.bfloat16)


def kernel(
    half,
    gate_hbm,
    up_hbm,
    codes_hbm,
    scale_hbm,
    turn_hbm,
    out_ref,
    scale,
    turn,
    gate,
    up,
    codes,
    hidden,
    gathered,
    turned,
    rot,
    levels,
    first,
    part,
    from_below_a,
    from_above_a,
    far_below,
    far_above,
    from_below_b,
    from_above_b,
    from_owners,
    load_sem,
    code_sem,
    gather_send,
    gather_recv,
    scatter_send,
    scatter_recv,
    a_send,
    a_recv,
    b_send,
    b_recv,
    c_send,
    c_recv,
):
    rows, hidden_width = gate.shape
    features = levels.shape[1]
    supers = hidden_width // SUPER
    piece = rows // SHARDS
    chunks = features // WIDTH
    dp = lax.axis_index("dp")
    me = lax.axis_index("tensor")
    rest = lax.rem(dp, half)
    y = lax.div(me, RUN)
    z_lo = lax.rem(me, RUN)
    z = lax.div(dp, half) * RUN + z_lo
    z_far = lax.rem(z + 6 - 4 * lax.div(z_lo, 2), NZ)
    z_of = (z, lax.rem(z + 1, NZ), lax.rem(z + NZ - 1, NZ), z_far)
    slot_there = (0, 2, 1, 3)

    def device(y_there, z_there):
        return (lax.div(z_there, RUN) * half + rest, y_there * RUN + lax.rem(z_there, RUN))

    def y_of(apart):
        return lax.rem(y + apart, NY)

    def wait_for(ref, sem):
        pltpu.make_async_copy(ref, ref, sem).wait()

    def send(src, dst, send_sem, recv_sem, where):
        pltpu.make_async_remote_copy(
            src_ref=src, dst_ref=dst, send_sem=send_sem, recv_sem=recv_sem, device_id=where, device_id_type=MESH
        ).start()

    barrier = pltpu.get_barrier_semaphore()

    def greet(apart, carry):
        pl.semaphore_signal(barrier, inc=1, device_id=(dp, lax.rem(me + apart, SHARDS)), device_id_type=MESH)
        return carry

    def input_copies(q):
        span = pl.ds(pl.multiple_of(q * SUPER, 128), SUPER)
        return (
            pltpu.make_async_copy(gate_hbm.at[:, span], gate.at[:, span], load_sem.at[0, q]),
            pltpu.make_async_copy(up_hbm.at[:, span], up.at[:, span], load_sem.at[1, q]),
        )

    for q in range(supers):
        for copy in input_copies(q):
            copy.start()
    load_turn = pltpu.make_async_copy(turn_hbm, turn, load_sem.at[2, 0])
    load_scale = pltpu.make_async_copy(scale_hbm, scale, load_sem.at[2, 1])
    load_turn.start()
    load_scale.start()
    lax.fori_loop(1, SHARDS, greet, 0)
    for slot in (1, 2, 3):

        @pl.when(lax.div(z_of[slot], RUN) != lax.div(z, RUN))
        def _(slot=slot):
            def greet_across(apart, carry):
                pl.semaphore_signal(
                    barrier, inc=1, device_id=device(y_of(apart), z_of[slot]), device_id_type=MESH
                )
                return carry

            lax.fori_loop(0, NY, greet_across, 0)

    def code_copy(q):
        span = pl.ds(pl.multiple_of(q * CODE_ROWS, CODE_ROWS), CODE_ROWS)
        return pltpu.make_async_copy(codes_hbm.at[span, :], codes.at[span, :], code_sem.at[q])

    across = 1 + lax.rem(lax.div(z_lo + 1, 2) + 1, 2)
    pl.semaphore_wait(barrier, SHARDS - 1 + NY * across)

    def send_hidden(q, carry):
        span = pl.ds(pl.multiple_of(q * SUPER, 128), SUPER)
        for copy in input_copies(q):
            copy.wait()

        def hidden_of(owner):
            its = pl.ds(pl.multiple_of(owner * piece, piece), piece)
            g = gate[its, span].astype(jnp.float32)
            value = g / (1.0 + jnp.exp(-g)) * up[its, span].astype(jnp.float32)
            return its, value.astype(jnp.bfloat16)

        mine = pl.ds(pl.multiple_of(me * piece, piece), piece)
        for apart in range(1, SHARDS):
            owner = lax.rem(me + apart, SHARDS)
            its, value = hidden_of(owner)
            hidden[its, span] = value
            send(
                hidden.at[its, span], gathered.at[mine, span], gather_send, gather_recv.at[q], (dp, owner)
            )
        its, value = hidden_of(me)
        gathered[its, span] = value
        return carry

    lax.fori_loop(0, supers, send_hidden, 0)
    for q in range(supers):
        code_copy(q).start()
    load_turn.wait()
    load_scale.wait()

    def decode_levels(q):
        code_copy(q).wait()

        def decode(tile, inner):
            columns = pl.ds(pl.multiple_of(tile * 256, 256), 256)
            code_span = pl.ds(pl.multiple_of(q * CODE_ROWS, CODE_ROWS), CODE_ROWS)
            shifted = codes[code_span, columns].astype(jnp.int32) + 8388608
            for digit in range(6):
                value = jnp.bitwise_and(jnp.right_shift(shifted, 4 * digit), 15) - 8
                level_span = pl.ds(pl.multiple_of(q * SUPER + digit * CODE_ROWS, CODE_ROWS), CODE_ROWS)
                levels[level_span, columns] = value.astype(jnp.float32).astype(jnp.bfloat16)
            return inner

        lax.fori_loop(0, features // 256, decode, 0)

    def rotate(q, carry):
        span = pl.ds(pl.multiple_of(q * SUPER, 128), SUPER)
        pl.when(q < supers - 1)(lambda: decode_levels(q))
        wait_for(gathered.at[pl.ds(0, (SHARDS - 1) * piece), span], gather_recv.at[q])
        local = jnp.dot(gathered[:, span], turn[...], preferred_element_type=jnp.float32)
        terms = [local[piece * t : piece * (t + 1)] for t in range(SHARDS)]
        step = 1
        while step < SHARDS:
            after = list(terms)
            for t in range(SHARDS):
                if not t & step:
                    after[t] = terms[t] + terms[t + step]
                    after[t + step] = terms[t] - terms[t + step]
            terms, step = after, 2 * step
        scaling = 1.0 / math.sqrt(128 * SHARDS)
        for t in range(SHARDS):
            turned[piece * t : piece * (t + 1), span] = (terms[t] * scaling).astype(jnp.bfloat16)
        for slot in (3, 1, 2, 0):
            for apart in (2, 1, 3, 0):
                if slot == 0 and apart == 0:
                    continue
                shard = y_of(apart) * RUN + lax.rem(z_of[slot], RUN)
                row = (((NY - apart) % NY) * 4 + slot_there[slot]) * piece
                send(
                    turned.at[pl.ds(pl.multiple_of(shard * piece, piece), piece), span],
                    rot.at[pl.ds(row, piece), span],
                    scatter_send,
                    scatter_recv.at[q],
                    device(y_of(apart), z_of[slot]),
                )
        rot[0:piece, span] = turned[pl.ds(pl.multiple_of(me * piece, piece), piece), span]
        return carry

    lax.fori_loop(0, supers, rotate, 0)
    decode_levels(supers - 1)

    def wait_rotated(q, carry):
        span = pl.ds(pl.multiple_of(q * SUPER, 128), SUPER)
        wait_for(rot.at[pl.ds(0, (SHARDS - 1) * piece), span], scatter_recv.at[q])
        first[...] += jnp.dot(
            rot[:, span], levels[span, 0 : FIRST * WIDTH], preferred_element_type=jnp.float32
        )
        return carry

    first[...] = jnp.zeros_like(first)
    lax.fori_loop(0, supers, wait_rotated, 0)

    def y_columns(c):
        t, kind = c
        return pl.ds(pl.multiple_of((t * PERIOD + kind) * WIDTH, 128), PATTERN[kind][0])

    def z_columns(c):
        t, kind = c
        return pl.ds(pl.multiple_of((t * PERIOD + kind) * WIDTH + PATTERN[kind][0], 128), PATTERN[kind][1])

    def far_columns(c):
        t, kind = c
        return pl.ds(pl.multiple_of(t * Z_SPAN + sum(z for _, z in PATTERN[:kind]), 128), PATTERN[kind][1])

    def index(c):
        return c[0] * PERIOD + c[1]

    def added(*values):
        total = values[0].astype(jnp.float32)
        for value in values[1:]:
            total = total + value.astype(jnp.float32)
        return total.astype(jnp.bfloat16)

    def rows_at(first, count):
        return pl.ds(first * piece, count * piece)

    y_above, y_below, y_across = (device(y_of(apart), z) for apart in (1, 3, 2))
    z_above, z_below, z_across = (device(y, z_of[slot]) for slot in (1, 2, 3))
    far_goes_down = z_lo < 2
    far_passes = lax.rem(z_lo, 3) == 0

    def multiply(c):
        columns = pl.ds(pl.multiple_of(index(c) * WIDTH, 128), WIDTH)
        start(c, jnp.dot(rot[...], levels[:, columns], preferred_element_type=jnp.float32))

    def start(c, product):
        columns = pl.ds(pl.multiple_of(index(c) * WIDTH, 128), WIDTH)
        product = (product * scale[:, columns]).astype(jnp.bfloat16)
        y_width = PATTERN[c[1]][0]
        part[:, y_columns(c)] = product[:, :y_width]
        for apart in range(NY):
            for slot in range(4):
                row = (apart * 4 + slot) * piece
                part[rows_at(slot * NY + apart, 1), z_columns(c)] = product[row : row + piece, y_width:]

        @pl.when(far_goes_down)
        def _():
            send(part.at[rows_at(12, 4), z_columns(c)], far_above.at[:, far_columns(c)], a_send, a_recv.at[3, index(c)], z_below)

        @pl.when(jnp.logical_not(far_goes_down))
        def _():
            send(part.at[rows_at(12, 4), z_columns(c)], far_below.at[:, far_columns(c)], a_send, a_recv.at[2, index(c)], z_above)

        send(part.at[rows_at(8, 2), y_columns(c)], from_below_a.at[:, y_columns(c)], a_send, a_recv.at[0, index(c)], y_above)
        send(part.at[rows_at(10, 2), y_columns(c)], from_above_a.at[:, y_columns(c)], a_send, a_recv.at[1, index(c)], y_below)

    def pass_on(c):
        @pl.when(far_passes)
        def _():
            wait_for(far_below.at[:, far_columns(c)], a_recv.at[2, index(c)])
            part[rows_at(4, 4), z_columns(c)] = added(part[rows_at(4, 4), z_columns(c)], far_below[:, far_columns(c)])
            wait_for(far_above.at[:, far_columns(c)], a_recv.at[3, index(c)])
            part[rows_at(8, 4), z_columns(c)] = added(part[rows_at(8, 4), z_columns(c)], far_above[:, far_columns(c)])

        send(part.at[rows_at(4, 4), z_columns(c)], from_below_b.at[:, z_columns(c)], b_send, b_recv.at[2, index(c)], z_above)
        send(part.at[rows_at(8, 4), z_columns(c)], from_above_b.at[:, z_columns(c)], b_send, b_recv.at[3, index(c)], z_below)
        wait_for(from_below_a.at[:, y_columns(c)], a_recv.at[0, index(c)])
        part[rows_at(4, 2), y_columns(c)] = added(part[rows_at(4, 2), y_columns(c)], from_below_a[:, y_columns(c)])
        send(part.at[rows_at(4, 4), y_columns(c)], from_below_b.at[:, y_columns(c)], b_send, b_recv.at[0, index(c)], y_above)
        wait_for(from_above_a.at[:, y_columns(c)], a_recv.at[1, index(c)])
        part[rows_at(14, 2), y_columns(c)] = added(part[rows_at(14, 2), y_columns(c)], from_above_a[:, y_columns(c)])
        send(part.at[rows_at(12, 4), y_columns(c)], from_above_b.at[:, y_columns(c)], b_send, b_recv.at[1, index(c)], y_below)

    def to_owners(c):
        def summed(columns, low):
            wait_for(from_below_b.at[:, columns], b_recv.at[low, index(c)])
            wait_for(from_above_b.at[:, columns], b_recv.at[low + 1, index(c)])
            part[rows_at(0, 4), columns] = added(
                part[rows_at(0, 4), columns], from_below_b[:, columns], from_above_b[:, columns]
            )

        def give(row, place, columns, sem, where):
            send(part.at[rows_at(row, 1), columns], from_owners.at[rows_at(place, 1), columns], c_send, c_recv.at[sem, index(c)], where)

        summed(z_columns(c), 2)
        give(2, 1, z_columns(c), 4, y_across)
        give(1, 0, z_columns(c), 3, y_above)
        give(3, 2, z_columns(c), 5, y_below)
        summed(y_columns(c), 0)
        give(3, 1, y_columns(c), 1, z_across)
        give(1, 0, y_columns(c), 0, z_above)
        give(2, 2, y_columns(c), 2, z_below)

    def finish(c):
        for columns, low in ((y_columns(c), 0), (z_columns(c), 3)):
            for place in range(3):
                wait_for(from_owners.at[rows_at(place, 1), columns], c_recv.at[low + place, index(c)])
            out_ref[:, columns] = added(
                part[rows_at(0, 1), columns], *(from_owners[rows_at(place, 1), columns] for place in range(3))
            )

    def step(t, carry):
        for kind in range(PERIOD):
            for lag, work in ((0, multiply), (LAG_B, pass_on), (LAG_C, to_owners), (LAG_D, finish)):
                chunk = (t + (kind - lag) // PERIOD, (kind - lag) % PERIOD)
                at = index(chunk)
                lowest = FIRST if lag == 0 else 0
                pl.when((at >= lowest) & (at < chunks))(functools.partial(work, chunk))
        return carry

    for kind in range(FIRST):
        start((0, kind), first[:, kind * WIDTH : (kind + 1) * WIDTH])
    lax.fori_loop(0, (chunks + LAG_D + PERIOD - 1) // PERIOD, step, 0)

    wait_for(gathered.at[pl.ds(0, (SHARDS - 1) * piece), :], gather_send)
    wait_for(rot.at[pl.ds(0, (SHARDS - 1) * piece), :], scatter_send)
    wait_for(part.at[rows_at(0, 4), :], a_send)
    wait_for(part.at[rows_at(0, 8), :], b_send)
    wait_for(from_owners, c_send)


def body(gate_inputs, up_inputs, down_codes, column_scale, half):
    rows, hidden_width = gate_inputs.shape
    code_rows, features = down_codes.shape
    chunks = features // WIDTH
    supers = hidden_width // SUPER
    piece, block = rows // SHARDS, rows // NY
    outside = pl.BlockSpec(memory_space=pl.ANY)
    b16 = jnp.bfloat16
    return pl.pallas_call(
        functools.partial(kernel, half),
        out_shape=jax.ShapeDtypeStruct((piece, features), b16),
        in_specs=[outside] * 5,
        out_specs=pl.BlockSpec(memory_space=pltpu.VMEM),
        scratch_shapes=[
            pltpu.VMEM((1, features), jnp.float32),
            pltpu.VMEM((SUPER, SUPER), b16),
            pltpu.VMEM((rows, hidden_width), b16),
            pltpu.VMEM((rows, hidden_width), b16),
            pltpu.VMEM((code_rows, features), jnp.float32),
            pltpu.VMEM((rows, hidden_width), b16),
            pltpu.VMEM((rows, hidden_width), b16),
            pltpu.VMEM((rows, hidden_width), b16),
            pltpu.VMEM((rows, hidden_width), b16),
            pltpu.VMEM((hidden_width, features), b16),
            pltpu.VMEM((rows, FIRST * WIDTH), jnp.float32),
            pltpu.VMEM((rows, features), b16),
            pltpu.VMEM((block // 2, features), b16),
            pltpu.VMEM((block // 2, features), b16),
            pltpu.VMEM((block, chunks // PERIOD * Z_SPAN), b16),
            pltpu.VMEM((block, chunks // PERIOD * Z_SPAN), b16),
            pltpu.VMEM((block, features), b16),
            pltpu.VMEM((block, features), b16),
            pltpu.VMEM((3 * piece, features), b16),
            pltpu.SemaphoreType.DMA((3, supers)),
            pltpu.SemaphoreType.DMA((supers,)),
            pltpu.SemaphoreType.DMA,
            pltpu.SemaphoreType.DMA((supers,)),
            pltpu.SemaphoreType.DMA,
            pltpu.SemaphoreType.DMA((supers,)),
            pltpu.SemaphoreType.DMA,
            pltpu.SemaphoreType.DMA((4, chunks)),
            pltpu.SemaphoreType.DMA,
            pltpu.SemaphoreType.DMA((4, chunks)),
            pltpu.SemaphoreType.DMA,
            pltpu.SemaphoreType.DMA((6, chunks)),
        ],
        compiler_params=pltpu.CompilerParams(
            collective_id=0, has_side_effects=True, vmem_limit_bytes=60 * 1024 * 1024
        ),
    )(gate_inputs, up_inputs, down_codes, column_scale.reshape(1, features), jnp.asarray(turn_matrix()))


def solution(mesh):
    return jax.shard_map(
        functools.partial(body, half=mesh.shape["dp"] // 2),
        mesh=mesh,
        in_specs=(P("dp", "tensor"), P("dp", "tensor"), P("tensor", None), P()),
        out_specs=P(("dp", "tensor"), None),
        check_vma=False,
    )
```

```python
import functools
import math

import jax
import jax.numpy as jnp
import ml_dtypes
import numpy as np
from jax import lax
from jax.experimental import pallas as pl
from jax.experimental.pallas import tpu as pltpu
from jax.sharding import PartitionSpec as P

MESH = pl.DeviceIdType.MESH
NY, NZ, RUN = 4, 8, 4
SHARDS = NY * RUN
SUPER = 384
CODE_ROWS = SUPER // 6
PATTERN = ((384, 128), (256, 256))
PERIOD = len(PATTERN)
WIDTH = sum(PATTERN[0])
DIRECT = 4
FIRST = 2
Z_SPAN = sum(z_width for _, z_width in PATTERN)
LAGS = 4, 8, 12, 16


def sylvester(extent):
    indices = np.arange(extent)
    common = indices[:, None] & indices[None, :]
    parity = np.zeros((extent, extent), np.int64)
    for offset in range(extent.bit_length() - 1):
        parity += (common >> offset) & 1
    return 1 - 2 * (parity % 2)


def turn_matrix():
    blocks = np.kron(np.eye(SUPER // 128), sylvester(128))
    order = np.arange(SUPER).reshape(CODE_ROWS, 6).T.reshape(-1)
    return blocks[:, order].astype(ml_dtypes.bfloat16)


def kernel(
    half,
    gate_hbm,
    up_hbm,
    codes_hbm,
    scale_hbm,
    turn_hbm,
    out_ref,
    scale,
    turn,
    gate,
    up,
    codes,
    hidden,
    gathered,
    turned,
    rot,
    levels,
    first,
    part,
    from_below_a,
    from_above_a,
    far_below,
    far_above,
    from_below_b,
    from_above_b,
    from_below_c,
    from_above_c,
    from_next,
    load_sem,
    code_sem,
    gather_send,
    gather_recv,
    scatter_send,
    scatter_recv,
    a_send,
    a_recv,
    b_send,
    b_recv,
    c_send,
    c_recv,
    d_send,
    e_send,
    d_recv,
):
    rows, hidden_width = gate.shape
    features = levels.shape[1]
    supers = hidden_width // SUPER
    piece = rows // SHARDS
    chunks = features // WIDTH
    dp = lax.axis_index("dp")
    me = lax.axis_index("tensor")
    rest = lax.rem(dp, half)
    y = lax.div(me, RUN)
    z_lo = lax.rem(me, RUN)
    z = lax.div(dp, half) * RUN + z_lo
    z_far = lax.rem(z + 6 - 4 * lax.div(z_lo, 2), NZ)
    z_of = (z, lax.rem(z + 1, NZ), lax.rem(z + NZ - 1, NZ), z_far)
    slot_there = (0, 2, 1, 3)

    def device(y_there, z_there):
        return (lax.div(z_there, RUN) * half + rest, y_there * RUN + lax.rem(z_there, RUN))

    def y_of(apart):
        return lax.rem(y + apart, NY)

    def wait_for(ref, sem):
        pltpu.make_async_copy(ref, ref, sem).wait()

    def send(src, dst, send_sem, recv_sem, where):
        pltpu.make_async_remote_copy(
            src_ref=src, dst_ref=dst, send_sem=send_sem, recv_sem=recv_sem, device_id=where, device_id_type=MESH
        ).start()

    barrier = pltpu.get_barrier_semaphore()

    def greet(apart, carry):
        pl.semaphore_signal(barrier, inc=1, device_id=(dp, lax.rem(me + apart, SHARDS)), device_id_type=MESH)
        return carry

    def input_copies(q):
        span = pl.ds(pl.multiple_of(q * SUPER, 128), SUPER)
        return (
            pltpu.make_async_copy(gate_hbm.at[:, span], gate.at[:, span], load_sem.at[0, q]),
            pltpu.make_async_copy(up_hbm.at[:, span], up.at[:, span], load_sem.at[1, q]),
        )

    for q in range(supers):
        for copy in input_copies(q):
            copy.start()
    load_turn = pltpu.make_async_copy(turn_hbm, turn, load_sem.at[2, 0])
    load_scale = pltpu.make_async_copy(scale_hbm, scale, load_sem.at[2, 1])
    load_turn.start()
    load_scale.start()
    lax.fori_loop(1, SHARDS, greet, 0)
    for slot in (1, 2, 3):

        @pl.when(lax.div(z_of[slot], RUN) != lax.div(z, RUN))
        def _(slot=slot):
            def greet_across(apart, carry):
                pl.semaphore_signal(
                    barrier, inc=1, device_id=device(y_of(apart), z_of[slot]), device_id_type=MESH
                )
                return carry

            lax.fori_loop(0, NY, greet_across, 0)

    def code_copy(q):
        span = pl.ds(pl.multiple_of(q * CODE_ROWS, CODE_ROWS), CODE_ROWS)
        return pltpu.make_async_copy(codes_hbm.at[span, :], codes.at[span, :], code_sem.at[q])

    across = 1 + lax.rem(lax.div(z_lo + 1, 2) + 1, 2)
    pl.semaphore_wait(barrier, SHARDS - 1 + NY * across)

    def send_hidden(q, carry):
        span = pl.ds(pl.multiple_of(q * SUPER, 128), SUPER)
        for copy in input_copies(q):
            copy.wait()

        def hidden_of(owner):
            its = pl.ds(pl.multiple_of(owner * piece, piece), piece)
            g = gate[its, span].astype(jnp.float32)
            value = g / (1.0 + jnp.exp(-g)) * up[its, span].astype(jnp.float32)
            return its, value.astype(jnp.bfloat16)

        mine = pl.ds(pl.multiple_of(me * piece, piece), piece)
        for apart in range(1, SHARDS):
            owner = lax.rem(me + apart, SHARDS)
            its, value = hidden_of(owner)
            hidden[its, span] = value
            send(
                hidden.at[its, span], gathered.at[mine, span], gather_send, gather_recv.at[q], (dp, owner)
            )
        its, value = hidden_of(me)
        gathered[its, span] = value
        return carry

    lax.fori_loop(0, supers, send_hidden, 0)
    for q in range(supers):
        code_copy(q).start()
    load_turn.wait()
    load_scale.wait()

    def decode_levels(q):
        code_copy(q).wait()

        def decode(tile, inner):
            columns = pl.ds(pl.multiple_of(tile * 256, 256), 256)
            code_span = pl.ds(pl.multiple_of(q * CODE_ROWS, CODE_ROWS), CODE_ROWS)
            shifted = codes[code_span, columns].astype(jnp.int32) + 8388608
            for digit in range(6):
                value = jnp.bitwise_and(jnp.right_shift(shifted, 4 * digit), 15) - 8
                level_span = pl.ds(pl.multiple_of(q * SUPER + digit * CODE_ROWS, CODE_ROWS), CODE_ROWS)
                levels[level_span, columns] = value.astype(jnp.float32).astype(jnp.bfloat16)
            return inner

        lax.fori_loop(0, features // 256, decode, 0)

    def rotate(q, carry):
        span = pl.ds(pl.multiple_of(q * SUPER, 128), SUPER)
        pl.when(q < supers - 1)(lambda: decode_levels(q))
        wait_for(gathered.at[pl.ds(0, (SHARDS - 1) * piece), span], gather_recv.at[q])
        local = jnp.dot(gathered[:, span], turn[...], preferred_element_type=jnp.float32)
        terms = [local[piece * t : piece * (t + 1)] for t in range(SHARDS)]
        step = 1
        while step < SHARDS:
            after = list(terms)
            for t in range(SHARDS):
                if not t & step:
                    after[t] = terms[t] + terms[t + step]
                    after[t + step] = terms[t] - terms[t + step]
            terms, step = after, 2 * step
        scaling = 1.0 / math.sqrt(128 * SHARDS)
        for t in range(SHARDS):
            turned[piece * t : piece * (t + 1), span] = (terms[t] * scaling).astype(jnp.bfloat16)
        for slot in (3, 1, 2, 0):
            for apart in (2, 1, 3, 0):
                if slot == 0 and apart == 0:
                    continue
                shard = y_of(apart) * RUN + lax.rem(z_of[slot], RUN)
                row = (((NY - apart) % NY) * 4 + slot_there[slot]) * piece
                send(
                    turned.at[pl.ds(pl.multiple_of(shard * piece, piece), piece), span],
                    rot.at[pl.ds(row, piece), span],
                    scatter_send,
                    scatter_recv.at[q],
                    device(y_of(apart), z_of[slot]),
                )
        rot[0:piece, span] = turned[pl.ds(pl.multiple_of(me * piece, piece), piece), span]
        return carry

    lax.fori_loop(0, supers, rotate, 0)
    decode_levels(supers - 1)

    def wait_rotated(q, carry):
        span = pl.ds(pl.multiple_of(q * SUPER, 128), SUPER)
        wait_for(rot.at[pl.ds(0, (SHARDS - 1) * piece), span], scatter_recv.at[q])
        first[...] += jnp.dot(
            rot[:, span], levels[span, 0 : FIRST * WIDTH], preferred_element_type=jnp.float32
        )
        return carry

    first[...] = jnp.zeros_like(first)
    lax.fori_loop(0, supers, wait_rotated, 0)

    def y_columns(c):
        t, kind = c
        return pl.ds(pl.multiple_of((t * PERIOD + kind) * WIDTH, 128), PATTERN[kind][0])

    def z_columns(c):
        t, kind = c
        return pl.ds(pl.multiple_of((t * PERIOD + kind) * WIDTH + PATTERN[kind][0], 128), PATTERN[kind][1])

    def far_columns(c):
        t, kind = c
        return pl.ds(pl.multiple_of(t * Z_SPAN + sum(z for _, z in PATTERN[:kind]), 128), PATTERN[kind][1])

    def index(c):
        return c[0] * PERIOD + c[1]

    shared_chunks = max(chunks - DIRECT, 0)

    def added(*values):
        total = values[0].astype(jnp.float32)
        for value in values[1:]:
            total = total + value.astype(jnp.float32)
        return total.astype(jnp.bfloat16)

    def rows_at(first, count):
        return pl.ds(first * piece, count * piece)

    y_above, y_below, y_across = (device(y_of(apart), z) for apart in (1, 3, 2))
    z_above, z_below, z_across = (device(y, z_of[slot]) for slot in (1, 2, 3))
    far_goes_down = z_lo < 2
    far_passes = lax.rem(z_lo, 3) == 0

    def multiply(c):
        columns = pl.ds(pl.multiple_of(index(c) * WIDTH, 128), WIDTH)
        start(c, jnp.dot(rot[...], levels[:, columns], preferred_element_type=jnp.float32))

    def start(c, product):
        columns = pl.ds(pl.multiple_of(index(c) * WIDTH, 128), WIDTH)
        product = (product * scale[:, columns]).astype(jnp.bfloat16)
        y_width = PATTERN[c[1]][0]
        part[:, y_columns(c)] = product[:, :y_width]
        for apart in range(NY):
            for slot in range(4):
                row = (apart * 4 + slot) * piece
                part[rows_at(slot * NY + apart, 1), z_columns(c)] = product[row : row + piece, y_width:]

        @pl.when(far_goes_down)
        def _():
            send(part.at[rows_at(12, 4), z_columns(c)], far_above.at[:, far_columns(c)], a_send, a_recv.at[3, index(c)], z_below)

        @pl.when(jnp.logical_not(far_goes_down))
        def _():
            send(part.at[rows_at(12, 4), z_columns(c)], far_below.at[:, far_columns(c)], a_send, a_recv.at[2, index(c)], z_above)

        send(part.at[rows_at(8, 2), y_columns(c)], from_below_a.at[:, y_columns(c)], a_send, a_recv.at[0, index(c)], y_above)
        send(part.at[rows_at(10, 2), y_columns(c)], from_above_a.at[:, y_columns(c)], a_send, a_recv.at[1, index(c)], y_below)

    def pass_on(c):
        @pl.when(far_passes)
        def _():
            wait_for(far_below.at[:, far_columns(c)], a_recv.at[2, index(c)])
            part[rows_at(4, 4), z_columns(c)] = added(part[rows_at(4, 4), z_columns(c)], far_below[:, far_columns(c)])
            wait_for(far_above.at[:, far_columns(c)], a_recv.at[3, index(c)])
            part[rows_at(8, 4), z_columns(c)] = added(part[rows_at(8, 4), z_columns(c)], far_above[:, far_columns(c)])

        send(part.at[rows_at(4, 4), z_columns(c)], from_below_b.at[:, z_columns(c)], b_send, b_recv.at[2, index(c)], z_above)
        send(part.at[rows_at(8, 4), z_columns(c)], from_above_b.at[:, z_columns(c)], b_send, b_recv.at[3, index(c)], z_below)
        wait_for(from_below_a.at[:, y_columns(c)], a_recv.at[0, index(c)])
        part[rows_at(4, 2), y_columns(c)] = added(part[rows_at(4, 2), y_columns(c)], from_below_a[:, y_columns(c)])
        send(part.at[rows_at(4, 4), y_columns(c)], from_below_b.at[:, y_columns(c)], b_send, b_recv.at[0, index(c)], y_above)
        wait_for(from_above_a.at[:, y_columns(c)], a_recv.at[1, index(c)])
        part[rows_at(14, 2), y_columns(c)] = added(part[rows_at(14, 2), y_columns(c)], from_above_a[:, y_columns(c)])
        send(part.at[rows_at(12, 4), y_columns(c)], from_above_b.at[:, y_columns(c)], b_send, b_recv.at[1, index(c)], y_below)

    def to_owners(c):
        def summed(columns, low):
            wait_for(from_below_b.at[:, columns], b_recv.at[low, index(c)])
            wait_for(from_above_b.at[:, columns], b_recv.at[low + 1, index(c)])
            part[rows_at(0, 4), columns] = added(
                part[rows_at(0, 4), columns], from_below_b[:, columns], from_above_b[:, columns]
            )

        def give(row, buffer, columns, sem, where):
            send(part.at[rows_at(row, 1), columns], buffer.at[:, columns], c_send, c_recv.at[sem, index(c)], where)

        shared = index(c) < shared_chunks
        summed(z_columns(c), 2)

        @pl.when(shared)
        def _():
            if c[1] % 2 == 0:
                give(2, from_below_c, z_columns(c), 2, y_above)
            else:
                give(2, from_above_c, z_columns(c), 2, y_below)

        @pl.when(jnp.logical_not(shared))
        def _():
            give_last(c, 2, 2, z_columns(c), 5, y_across, e_send)
            give_last(c, 1, 0, z_columns(c), 2, y_above, e_send)
            give_last(c, 3, 1, z_columns(c), 3, y_below, e_send)

        summed(y_columns(c), 0)

        @pl.when(shared)
        def _():
            pl.when(far_goes_down)(lambda: give(3, from_above_c, y_columns(c), 1, z_below))
            pl.when(jnp.logical_not(far_goes_down))(lambda: give(3, from_below_c, y_columns(c), 0, z_above))

        @pl.when(jnp.logical_not(shared))
        def _():
            give_last(c, 3, 2, y_columns(c), 4, z_across, e_send)
            give_last(c, 1, 0, y_columns(c), 0, z_above, e_send)
            give_last(c, 2, 1, y_columns(c), 1, z_below, e_send)

    def give_last(c, row, place, columns, sem, where, done):
        send(
            part.at[rows_at(row, 1), columns],
            from_next.at[rows_at(place, 1), columns],
            done,
            d_recv.at[sem, index(c)],
            where,
        )

    def last_hop(c):
        def add(row, buffer, columns, sem):
            wait_for(buffer.at[:, columns], c_recv.at[sem, index(c)])
            part[rows_at(row, 1), columns] = added(part[rows_at(row, 1), columns], buffer[:, columns])

        if c[1] % 2 == 0:
            add(1, from_below_c, z_columns(c), 2)
        else:
            add(3, from_above_c, z_columns(c), 2)
        give_last(c, 1, 0, z_columns(c), 2, y_above, d_send)
        give_last(c, 3, 1, z_columns(c), 3, y_below, d_send)

        @pl.when(far_passes)
        def _():
            add(1, from_below_c, y_columns(c), 0)
            add(2, from_above_c, y_columns(c), 1)

        give_last(c, 1, 0, y_columns(c), 0, z_above, d_send)
        give_last(c, 2, 1, y_columns(c), 1, z_below, d_send)

    def finish(c):
        def total(columns, sems):
            for place, sem in enumerate(sems):
                wait_for(from_next.at[rows_at(place, 1), columns], d_recv.at[sem, index(c)])
            out_ref[:, columns] = added(
                part[rows_at(0, 1), columns], *(from_next[rows_at(place, 1), columns] for place in range(len(sems)))
            )

        @pl.when(index(c) < shared_chunks)
        def _():
            total(y_columns(c), (0, 1))
            total(z_columns(c), (2, 3))

        @pl.when(index(c) >= shared_chunks)
        def _():
            total(y_columns(c), (0, 1, 4))
            total(z_columns(c), (2, 3, 5))

    def step(t, carry):
        for kind in range(PERIOD):
            for lag, work in zip((0, *LAGS), (multiply, pass_on, to_owners, last_hop, finish)):
                chunk = (t + (kind - lag) // PERIOD, (kind - lag) % PERIOD)
                at = index(chunk)
                lowest = FIRST if lag == 0 else 0
                highest = shared_chunks if work is last_hop else chunks
                pl.when((at >= lowest) & (at < highest))(functools.partial(work, chunk))
        return carry

    for kind in range(FIRST):
        start((0, kind), first[:, kind * WIDTH : (kind + 1) * WIDTH])
    lax.fori_loop(0, (chunks + LAGS[-1] + PERIOD - 1) // PERIOD, step, 0)

    wait_for(gathered.at[pl.ds(0, (SHARDS - 1) * piece), :], gather_send)
    wait_for(rot.at[pl.ds(0, (SHARDS - 1) * piece), :], scatter_send)
    wait_for(part.at[rows_at(0, 4), :], a_send)
    wait_for(part.at[rows_at(0, 8), :], b_send)
    split = shared_chunks * WIDTH
    if split:
        wait_for(part.at[rows_at(0, 1), 0:split], c_send)
        wait_for(from_next.at[rows_at(0, 2), 0:split], d_send)
    if split < features:
        wait_for(from_next.at[:, split:features], e_send)


def body(gate_inputs, up_inputs, down_codes, column_scale, half):
    rows, hidden_width = gate_inputs.shape
    code_rows, features = down_codes.shape
    chunks = features // WIDTH
    supers = hidden_width // SUPER
    piece, block = rows // SHARDS, rows // NY
    outside = pl.BlockSpec(memory_space=pl.ANY)
    b16 = jnp.bfloat16
    return pl.pallas_call(
        functools.partial(kernel, half),
        out_shape=jax.ShapeDtypeStruct((piece, features), b16),
        in_specs=[outside] * 5,
        out_specs=pl.BlockSpec(memory_space=pltpu.VMEM),
        scratch_shapes=[
            pltpu.VMEM((1, features), jnp.float32),
            pltpu.VMEM((SUPER, SUPER), b16),
            pltpu.VMEM((rows, hidden_width), b16),
            pltpu.VMEM((rows, hidden_width), b16),
            pltpu.VMEM((code_rows, features), jnp.float32),
            pltpu.VMEM((rows, hidden_width), b16),
            pltpu.VMEM((rows, hidden_width), b16),
            pltpu.VMEM((rows, hidden_width), b16),
            pltpu.VMEM((rows, hidden_width), b16),
            pltpu.VMEM((hidden_width, features), b16),
            pltpu.VMEM((rows, FIRST * WIDTH), jnp.float32),
            pltpu.VMEM((rows, features), b16),
            pltpu.VMEM((block // 2, features), b16),
            pltpu.VMEM((block // 2, features), b16),
            pltpu.VMEM((block, chunks // PERIOD * Z_SPAN), b16),
            pltpu.VMEM((block, chunks // PERIOD * Z_SPAN), b16),
            pltpu.VMEM((block, features), b16),
            pltpu.VMEM((block, features), b16),
            pltpu.VMEM((piece, features), b16),
            pltpu.VMEM((piece, features), b16),
            pltpu.VMEM((3 * piece, features), b16),
            pltpu.SemaphoreType.DMA((3, supers)),
            pltpu.SemaphoreType.DMA((supers,)),
            pltpu.SemaphoreType.DMA,
            pltpu.SemaphoreType.DMA((supers,)),
            pltpu.SemaphoreType.DMA,
            pltpu.SemaphoreType.DMA((supers,)),
            pltpu.SemaphoreType.DMA,
            pltpu.SemaphoreType.DMA((4, chunks)),
            pltpu.SemaphoreType.DMA,
            pltpu.SemaphoreType.DMA((4, chunks)),
            pltpu.SemaphoreType.DMA,
            pltpu.SemaphoreType.DMA((3, chunks)),
            pltpu.SemaphoreType.DMA,
            pltpu.SemaphoreType.DMA,
            pltpu.SemaphoreType.DMA((6, chunks)),
        ],
        compiler_params=pltpu.CompilerParams(
            collective_id=0, has_side_effects=True, vmem_limit_bytes=60 * 1024 * 1024
        ),
    )(gate_inputs, up_inputs, down_codes, column_scale.reshape(1, features), jnp.asarray(turn_matrix()))


def solution(mesh):
    return jax.shard_map(
        functools.partial(body, half=mesh.shape["dp"] // 2),
        mesh=mesh,
        in_specs=(P("dp", "tensor"), P("dp", "tensor"), P("tensor", None), P()),
        out_specs=P(("dp", "tensor"), None),
        check_vma=False,
    )
```

```python
import functools
import math

import jax
import jax.numpy as jnp
import ml_dtypes
import numpy as np
from jax import lax
from jax.experimental import pallas as pl
from jax.experimental.pallas import tpu as pltpu
from jax.sharding import PartitionSpec as P

MESH = pl.DeviceIdType.MESH
NY, NZ, RUN = 4, 8, 4
SHARDS = NY * RUN
SUPER = 384
CODE_ROWS = SUPER // 6
PATTERN = ((384, 128), (256, 256))
PERIOD = len(PATTERN)
WIDTH = sum(PATTERN[0])
DIRECT = 6
FIRST = 4
Z_SPAN = sum(z_width for _, z_width in PATTERN)
LAGS = 5, 9, 13, 17


def sylvester(extent):
    indices = np.arange(extent)
    common = indices[:, None] & indices[None, :]
    parity = np.zeros((extent, extent), np.int64)
    for offset in range(extent.bit_length() - 1):
        parity += (common >> offset) & 1
    return 1 - 2 * (parity % 2)


def turn_matrix():
    blocks = np.kron(np.eye(SUPER // 128), sylvester(128))
    order = np.arange(SUPER).reshape(CODE_ROWS, 6).T.reshape(-1)
    return blocks[:, order].astype(ml_dtypes.bfloat16)


def kernel(
    half,
    gate_hbm,
    up_hbm,
    codes_hbm,
    scale_hbm,
    turn_hbm,
    out_hbm,
    out,
    scale,
    turn,
    gate,
    up,
    codes,
    hidden,
    gathered,
    turned,
    rot,
    levels,
    first,
    part,
    from_below_a,
    from_above_a,
    far_below,
    far_above,
    from_below_b,
    from_above_b,
    from_below_c,
    from_above_c,
    from_next,
    out_sem,
    load_sem,
    code_sem,
    gather_send,
    gather_recv,
    scatter_send,
    scatter_recv,
    a_send,
    a_recv,
    b_send,
    b_recv,
    c_send,
    c_recv,
    d_send,
    e_send,
    d_recv,
):
    rows, hidden_width = gate.shape
    features = levels.shape[1]
    supers = hidden_width // SUPER
    piece = rows // SHARDS
    chunks = features // WIDTH
    dp = lax.axis_index("dp")
    me = lax.axis_index("tensor")
    rest = lax.rem(dp, half)
    y = lax.div(me, RUN)
    z_lo = lax.rem(me, RUN)
    z = lax.div(dp, half) * RUN + z_lo
    z_far = lax.rem(z + 6 - 4 * lax.div(z_lo, 2), NZ)
    z_of = (z, lax.rem(z + 1, NZ), lax.rem(z + NZ - 1, NZ), z_far)
    slot_there = (0, 2, 1, 3)

    def device(y_there, z_there):
        return (lax.div(z_there, RUN) * half + rest, y_there * RUN + lax.rem(z_there, RUN))

    def y_of(apart):
        return lax.rem(y + apart, NY)

    def wait_for(ref, sem):
        pltpu.make_async_copy(ref, ref, sem).wait()

    def send(src, dst, send_sem, recv_sem, where):
        pltpu.make_async_remote_copy(
            src_ref=src, dst_ref=dst, send_sem=send_sem, recv_sem=recv_sem, device_id=where, device_id_type=MESH
        ).start()

    barrier = pltpu.get_barrier_semaphore()

    def greet(apart, carry):
        pl.semaphore_signal(barrier, inc=1, device_id=(dp, lax.rem(me + apart, SHARDS)), device_id_type=MESH)
        return carry

    lax.fori_loop(1, SHARDS, greet, 0)
    for slot in (1, 2, 3):

        @pl.when(lax.div(z_of[slot], RUN) != lax.div(z, RUN))
        def _(slot=slot):
            def greet_across(apart, carry):
                pl.semaphore_signal(
                    barrier, inc=1, device_id=device(y_of(apart), z_of[slot]), device_id_type=MESH
                )
                return carry

            lax.fori_loop(0, NY, greet_across, 0)

    def input_copies(q):
        span = pl.ds(pl.multiple_of(q * SUPER, 128), SUPER)
        return (
            pltpu.make_async_copy(gate_hbm.at[:, span], gate.at[:, span], load_sem.at[0, q]),
            pltpu.make_async_copy(up_hbm.at[:, span], up.at[:, span], load_sem.at[1, q]),
        )

    for q in range(supers):
        for copy in input_copies(q):
            copy.start()
    load_turn = pltpu.make_async_copy(turn_hbm, turn, load_sem.at[2, 0])
    load_scale = pltpu.make_async_copy(scale_hbm, scale, load_sem.at[2, 1])
    load_turn.start()
    load_scale.start()
    def code_copy(q):
        span = pl.ds(pl.multiple_of(q * CODE_ROWS, CODE_ROWS), CODE_ROWS)
        return pltpu.make_async_copy(codes_hbm.at[span, :], codes.at[span, :], code_sem.at[q])

    across = 1 + lax.rem(lax.div(z_lo + 1, 2) + 1, 2)
    pl.semaphore_wait(barrier, SHARDS - 1 + NY * across)

    def send_hidden(q, carry):
        span = pl.ds(pl.multiple_of(q * SUPER, 128), SUPER)
        for copy in input_copies(q):
            copy.wait()

        def hidden_of(owner):
            its = pl.ds(pl.multiple_of(owner * piece, piece), piece)
            g = gate[its, span].astype(jnp.float32)
            value = g / (1.0 + jnp.exp(-g)) * up[its, span].astype(jnp.float32)
            return its, value.astype(jnp.bfloat16)

        mine = pl.ds(pl.multiple_of(me * piece, piece), piece)
        for apart in range(1, SHARDS):
            owner = lax.rem(me + apart, SHARDS)
            its, value = hidden_of(owner)
            hidden[its, span] = value
            send(
                hidden.at[its, span], gathered.at[mine, span], gather_send, gather_recv.at[q], (dp, owner)
            )
        its, value = hidden_of(me)
        gathered[its, span] = value
        return carry

    lax.fori_loop(0, supers, send_hidden, 0)
    for q in range(supers):
        code_copy(q).start()
    load_turn.wait()
    load_scale.wait()

    def decode_levels(q):
        code_copy(q).wait()

        def decode(tile, inner):
            columns = pl.ds(pl.multiple_of(tile * 256, 256), 256)
            code_span = pl.ds(pl.multiple_of(q * CODE_ROWS, CODE_ROWS), CODE_ROWS)
            shifted = codes[code_span, columns].astype(jnp.int32) + 8388608
            for digit in range(6):
                value = jnp.bitwise_and(jnp.right_shift(shifted, 4 * digit), 15) - 8
                level_span = pl.ds(pl.multiple_of(q * SUPER + digit * CODE_ROWS, CODE_ROWS), CODE_ROWS)
                levels[level_span, columns] = value.astype(jnp.float32).astype(jnp.bfloat16)
            return inner

        lax.fori_loop(0, features // 256, decode, 0)

    def rotate(q, carry):
        span = pl.ds(pl.multiple_of(q * SUPER, 128), SUPER)
        pl.when(q < supers - 1)(lambda: decode_levels(q))
        wait_for(gathered.at[pl.ds(0, (SHARDS - 1) * piece), span], gather_recv.at[q])
        local = jnp.dot(gathered[:, span], turn[...], preferred_element_type=jnp.float32)
        terms = [local[piece * t : piece * (t + 1)] for t in range(SHARDS)]
        step = 1
        while step < SHARDS:
            after = list(terms)
            for t in range(SHARDS):
                if not t & step:
                    after[t] = terms[t] + terms[t + step]
                    after[t + step] = terms[t] - terms[t + step]
            terms, step = after, 2 * step
        scaling = 1.0 / math.sqrt(128 * SHARDS)
        for t in range(SHARDS):
            turned[piece * t : piece * (t + 1), span] = (terms[t] * scaling).astype(jnp.bfloat16)
        for slot in (3, 1, 2, 0):
            for apart in (2, 1, 3, 0):
                if slot == 0 and apart == 0:
                    continue
                shard = y_of(apart) * RUN + lax.rem(z_of[slot], RUN)
                row = (((NY - apart) % NY) * 4 + slot_there[slot]) * piece
                send(
                    turned.at[pl.ds(pl.multiple_of(shard * piece, piece), piece), span],
                    rot.at[pl.ds(row, piece), span],
                    scatter_send,
                    scatter_recv.at[q],
                    device(y_of(apart), z_of[slot]),
                )
        rot[0:piece, span] = turned[pl.ds(pl.multiple_of(me * piece, piece), piece), span]
        return carry

    lax.fori_loop(0, supers, rotate, 0)
    decode_levels(supers - 1)

    def wait_rotated(q):
        span = pl.ds(pl.multiple_of(q * SUPER, 128), SUPER)
        wait_for(rot.at[pl.ds(0, (SHARDS - 1) * piece), span], scatter_recv.at[q])
        return span

    def grow(q, carry):
        span = wait_rotated(q)
        first[...] += jnp.dot(
            rot[:, span], levels[span, 0 : FIRST * WIDTH], preferred_element_type=jnp.float32
        )
        return carry

    first[...] = jnp.zeros_like(first)
    lax.fori_loop(0, supers - 1, grow, 0)
    last_span = wait_rotated(supers - 1)

    def y_columns(c):
        t, kind = c
        return pl.ds(pl.multiple_of((t * PERIOD + kind) * WIDTH, 128), PATTERN[kind][0])

    def z_columns(c):
        t, kind = c
        return pl.ds(pl.multiple_of((t * PERIOD + kind) * WIDTH + PATTERN[kind][0], 128), PATTERN[kind][1])

    def far_columns(c):
        t, kind = c
        return pl.ds(pl.multiple_of(t * Z_SPAN + sum(z for _, z in PATTERN[:kind]), 128), PATTERN[kind][1])

    def index(c):
        return c[0] * PERIOD + c[1]

    shared_chunks = max(chunks - DIRECT, 0)

    def added(*values):
        total = values[0].astype(jnp.float32)
        for value in values[1:]:
            total = total + value.astype(jnp.float32)
        return total.astype(jnp.bfloat16)

    def rows_at(first, count):
        return pl.ds(first * piece, count * piece)

    y_above, y_below, y_across = (device(y_of(apart), z) for apart in (1, 3, 2))
    z_above, z_below, z_across = (device(y, z_of[slot]) for slot in (1, 2, 3))
    far_goes_down = z_lo < 2
    far_passes = lax.rem(z_lo, 3) == 0

    def multiply(c):
        columns = pl.ds(pl.multiple_of(index(c) * WIDTH, 128), WIDTH)
        start(c, jnp.dot(rot[...], levels[:, columns], preferred_element_type=jnp.float32))

    def start(c, product):
        columns = pl.ds(pl.multiple_of(index(c) * WIDTH, 128), WIDTH)
        product = (product * scale[:, columns]).astype(jnp.bfloat16)
        y_width = PATTERN[c[1]][0]
        part[:, y_columns(c)] = product[:, :y_width]
        for apart in range(NY):
            for slot in range(4):
                row = (apart * 4 + slot) * piece
                part[rows_at(slot * NY + apart, 1), z_columns(c)] = product[row : row + piece, y_width:]

        @pl.when(far_goes_down)
        def _():
            send(part.at[rows_at(12, 4), z_columns(c)], far_above.at[:, far_columns(c)], a_send, a_recv.at[3, index(c)], z_below)

        @pl.when(jnp.logical_not(far_goes_down))
        def _():
            send(part.at[rows_at(12, 4), z_columns(c)], far_below.at[:, far_columns(c)], a_send, a_recv.at[2, index(c)], z_above)

        send(part.at[rows_at(8, 2), y_columns(c)], from_below_a.at[:, y_columns(c)], a_send, a_recv.at[0, index(c)], y_above)
        send(part.at[rows_at(10, 2), y_columns(c)], from_above_a.at[:, y_columns(c)], a_send, a_recv.at[1, index(c)], y_below)

    def pass_on(c):
        @pl.when(far_passes)
        def _():
            wait_for(far_below.at[:, far_columns(c)], a_recv.at[2, index(c)])
            part[rows_at(4, 4), z_columns(c)] = added(part[rows_at(4, 4), z_columns(c)], far_below[:, far_columns(c)])
            wait_for(far_above.at[:, far_columns(c)], a_recv.at[3, index(c)])
            part[rows_at(8, 4), z_columns(c)] = added(part[rows_at(8, 4), z_columns(c)], far_above[:, far_columns(c)])

        send(part.at[rows_at(4, 4), z_columns(c)], from_below_b.at[:, z_columns(c)], b_send, b_recv.at[2, index(c)], z_above)
        send(part.at[rows_at(8, 4), z_columns(c)], from_above_b.at[:, z_columns(c)], b_send, b_recv.at[3, index(c)], z_below)
        wait_for(from_below_a.at[:, y_columns(c)], a_recv.at[0, index(c)])
        part[rows_at(4, 2), y_columns(c)] = added(part[rows_at(4, 2), y_columns(c)], from_below_a[:, y_columns(c)])
        send(part.at[rows_at(4, 4), y_columns(c)], from_below_b.at[:, y_columns(c)], b_send, b_recv.at[0, index(c)], y_above)
        wait_for(from_above_a.at[:, y_columns(c)], a_recv.at[1, index(c)])
        part[rows_at(14, 2), y_columns(c)] = added(part[rows_at(14, 2), y_columns(c)], from_above_a[:, y_columns(c)])
        send(part.at[rows_at(12, 4), y_columns(c)], from_above_b.at[:, y_columns(c)], b_send, b_recv.at[1, index(c)], y_below)

    def to_owners(c):
        def summed(columns, low):
            wait_for(from_below_b.at[:, columns], b_recv.at[low, index(c)])
            wait_for(from_above_b.at[:, columns], b_recv.at[low + 1, index(c)])
            part[rows_at(0, 4), columns] = added(
                part[rows_at(0, 4), columns], from_below_b[:, columns], from_above_b[:, columns]
            )

        def give(row, buffer, columns, sem, where):
            send(part.at[rows_at(row, 1), columns], buffer.at[:, columns], c_send, c_recv.at[sem, index(c)], where)

        shared = index(c) < shared_chunks
        summed(z_columns(c), 2)

        @pl.when(shared)
        def _():
            if c[1] % 2 == 0:
                give(2, from_below_c, z_columns(c), 2, y_above)
            else:
                give(2, from_above_c, z_columns(c), 2, y_below)

        @pl.when(jnp.logical_not(shared))
        def _():
            give_last(c, 2, 2, z_columns(c), 5, y_across, e_send)
            give_last(c, 1, 0, z_columns(c), 2, y_above, e_send)
            give_last(c, 3, 1, z_columns(c), 3, y_below, e_send)

        summed(y_columns(c), 0)

        @pl.when(shared)
        def _():
            pl.when(far_goes_down)(lambda: give(3, from_above_c, y_columns(c), 1, z_below))
            pl.when(jnp.logical_not(far_goes_down))(lambda: give(3, from_below_c, y_columns(c), 0, z_above))

        @pl.when(jnp.logical_not(shared))
        def _():
            give_last(c, 3, 2, y_columns(c), 4, z_across, e_send)
            give_last(c, 1, 0, y_columns(c), 0, z_above, e_send)
            give_last(c, 2, 1, y_columns(c), 1, z_below, e_send)

    def give_last(c, row, place, columns, sem, where, done):
        send(
            part.at[rows_at(row, 1), columns],
            from_next.at[rows_at(place, 1), columns],
            done,
            d_recv.at[sem, index(c)],
            where,
        )

    def last_hop(c):
        def add(row, buffer, columns, sem):
            wait_for(buffer.at[:, columns], c_recv.at[sem, index(c)])
            part[rows_at(row, 1), columns] = added(part[rows_at(row, 1), columns], buffer[:, columns])

        if c[1] % 2 == 0:
            add(1, from_below_c, z_columns(c), 2)
        else:
            add(3, from_above_c, z_columns(c), 2)
        give_last(c, 1, 0, z_columns(c), 2, y_above, d_send)
        give_last(c, 3, 1, z_columns(c), 3, y_below, d_send)

        @pl.when(far_passes)
        def _():
            add(1, from_below_c, y_columns(c), 0)
            add(2, from_above_c, y_columns(c), 1)

        give_last(c, 1, 0, y_columns(c), 0, z_above, d_send)
        give_last(c, 2, 1, y_columns(c), 1, z_below, d_send)

    def finish(c):
        def total(columns, sems):
            for place, sem in enumerate(sems):
                wait_for(from_next.at[rows_at(place, 1), columns], d_recv.at[sem, index(c)])
            out[:, columns] = added(
                part[rows_at(0, 1), columns], *(from_next[rows_at(place, 1), columns] for place in range(len(sems)))
            )

        @pl.when(index(c) < shared_chunks)
        def _():
            total(y_columns(c), (0, 1))
            total(z_columns(c), (2, 3))

        @pl.when(index(c) >= shared_chunks)
        def _():
            total(y_columns(c), (0, 1, 4))
            total(z_columns(c), (2, 3, 5))

        columns = pl.ds(pl.multiple_of(index(c) * WIDTH, 128), WIDTH)
        pltpu.make_async_copy(out.at[:, columns], out_hbm.at[:, columns], out_sem).start()

    def step(t, carry):
        for kind in range(PERIOD):
            for lag, work in zip((*LAGS, 0), (pass_on, to_owners, last_hop, finish, multiply)):
                chunk = (t + (kind - lag) // PERIOD, (kind - lag) % PERIOD)
                at = index(chunk)
                lowest = FIRST if lag == 0 else 0
                highest = shared_chunks if work is last_hop else chunks
                pl.when((at >= lowest) & (at < highest))(functools.partial(work, chunk))
        return carry

    for kind in range(FIRST):
        columns = slice(kind * WIDTH, (kind + 1) * WIDTH)
        product = jnp.dot(rot[:, last_span], levels[last_span, columns], preferred_element_type=jnp.float32)
        start((kind // PERIOD, kind % PERIOD), first[:, columns] + product)
    lax.fori_loop(0, (chunks + LAGS[-1] + PERIOD - 1) // PERIOD, step, 0)

    wait_for(out, out_sem)
    wait_for(gathered.at[pl.ds(0, (SHARDS - 1) * piece), :], gather_send)
    wait_for(rot.at[pl.ds(0, (SHARDS - 1) * piece), :], scatter_send)
    wait_for(part.at[rows_at(0, 4), :], a_send)
    wait_for(part.at[rows_at(0, 8), :], b_send)
    split = shared_chunks * WIDTH
    if split:
        wait_for(part.at[rows_at(0, 1), 0:split], c_send)
        wait_for(from_next.at[rows_at(0, 2), 0:split], d_send)
    if split < features:
        wait_for(from_next.at[:, split:features], e_send)


def body(gate_inputs, up_inputs, down_codes, column_scale, half):
    rows, hidden_width = gate_inputs.shape
    code_rows, features = down_codes.shape
    chunks = features // WIDTH
    supers = hidden_width // SUPER
    piece, block = rows // SHARDS, rows // NY
    outside = pl.BlockSpec(memory_space=pl.ANY)
    b16 = jnp.bfloat16
    return pl.pallas_call(
        functools.partial(kernel, half),
        out_shape=jax.ShapeDtypeStruct((piece, features), b16),
        in_specs=[outside] * 5,
        out_specs=outside,
        scratch_shapes=[
            pltpu.VMEM((piece, features), b16),
            pltpu.VMEM((1, features), jnp.float32),
            pltpu.VMEM((SUPER, SUPER), b16),
            pltpu.VMEM((rows, hidden_width), b16),
            pltpu.VMEM((rows, hidden_width), b16),
            pltpu.VMEM((code_rows, features), jnp.float32),
            pltpu.VMEM((rows, hidden_width), b16),
            pltpu.VMEM((rows, hidden_width), b16),
            pltpu.VMEM((rows, hidden_width), b16),
            pltpu.VMEM((rows, hidden_width), b16),
            pltpu.VMEM((hidden_width, features), b16),
            pltpu.VMEM((rows, FIRST * WIDTH), jnp.float32),
            pltpu.VMEM((rows, features), b16),
            pltpu.VMEM((block // 2, features), b16),
            pltpu.VMEM((block // 2, features), b16),
            pltpu.VMEM((block, chunks // PERIOD * Z_SPAN), b16),
            pltpu.VMEM((block, chunks // PERIOD * Z_SPAN), b16),
            pltpu.VMEM((block, features), b16),
            pltpu.VMEM((block, features), b16),
            pltpu.VMEM((piece, features), b16),
            pltpu.VMEM((piece, features), b16),
            pltpu.VMEM((3 * piece, features), b16),
            pltpu.SemaphoreType.DMA,
            pltpu.SemaphoreType.DMA((3, supers)),
            pltpu.SemaphoreType.DMA((supers,)),
            pltpu.SemaphoreType.DMA,
            pltpu.SemaphoreType.DMA((supers,)),
            pltpu.SemaphoreType.DMA,
            pltpu.SemaphoreType.DMA((supers,)),
            pltpu.SemaphoreType.DMA,
            pltpu.SemaphoreType.DMA((4, chunks)),
            pltpu.SemaphoreType.DMA,
            pltpu.SemaphoreType.DMA((4, chunks)),
            pltpu.SemaphoreType.DMA,
            pltpu.SemaphoreType.DMA((3, chunks)),
            pltpu.SemaphoreType.DMA,
            pltpu.SemaphoreType.DMA,
            pltpu.SemaphoreType.DMA((6, chunks)),
        ],
        compiler_params=pltpu.CompilerParams(
            collective_id=0, has_side_effects=True, vmem_limit_bytes=60 * 1024 * 1024
        ),
    )(gate_inputs, up_inputs, down_codes, column_scale.reshape(1, features), jnp.asarray(turn_matrix()))


def solution(mesh):
    return jax.shard_map(
        functools.partial(body, half=mesh.shape["dp"] // 2),
        mesh=mesh,
        in_specs=(P("dp", "tensor"), P("dp", "tensor"), P("tensor", None), P()),
        out_specs=P(("dp", "tensor"), None),
        check_vma=False,
    )
```

```python
import functools
import math

import jax
import jax.numpy as jnp
import ml_dtypes
import numpy as np
from jax import lax
from jax.experimental import pallas as pl
from jax.experimental.pallas import tpu as pltpu
from jax.sharding import PartitionSpec as P

MESH = pl.DeviceIdType.MESH
NY, NZ, RUN = 4, 8, 4
SHARDS = NY * RUN
SUPER = 384
CODE_ROWS = SUPER // 6
PATTERN = ((384, 128), (256, 256))
PERIOD = len(PATTERN)
WIDTH = sum(PATTERN[0])
DIRECT = 6
FIRST = 4
Z_SPAN = sum(z_width for _, z_width in PATTERN)
LAGS = 5, 9, 13, 17


def sylvester(extent):
    indices = np.arange(extent)
    common = indices[:, None] & indices[None, :]
    parity = np.zeros((extent, extent), np.int64)
    for offset in range(extent.bit_length() - 1):
        parity += (common >> offset) & 1
    return 1 - 2 * (parity % 2)


def turn_matrix():
    blocks = np.kron(np.eye(SUPER // 128), sylvester(128))
    order = np.arange(SUPER).reshape(CODE_ROWS, 6).T.reshape(-1)
    return blocks[:, order].astype(ml_dtypes.bfloat16)


def kernel(
    half,
    gate_hbm,
    up_hbm,
    codes_hbm,
    scale_hbm,
    turn_hbm,
    out_hbm,
    out,
    scale,
    turn,
    gate,
    up,
    codes,
    hidden,
    gathered,
    turned,
    rot,
    levels,
    first,
    part,
    from_below_a,
    from_above_a,
    far_below,
    far_above,
    from_below_b,
    from_above_b,
    from_below_c,
    from_above_c,
    from_next,
    out_sem,
    load_sem,
    code_sem,
    gather_send,
    gather_recv,
    scatter_send,
    scatter_recv,
    a_send,
    a_recv,
    b_send,
    b_recv,
    c_send,
    c_recv,
    d_send,
    e_send,
    d_recv,
):
    rows, hidden_width = gate.shape
    features = levels.shape[1]
    supers = hidden_width // SUPER
    piece = rows // SHARDS
    chunks = features // WIDTH
    dp = lax.axis_index("dp")
    me = lax.axis_index("tensor")
    rest = lax.rem(dp, half)
    y = lax.div(me, RUN)
    z_lo = lax.rem(me, RUN)
    z = lax.div(dp, half) * RUN + z_lo
    z_far = lax.rem(z + 6 - 4 * lax.div(z_lo, 2), NZ)
    z_of = (z, lax.rem(z + 1, NZ), lax.rem(z + NZ - 1, NZ), z_far)
    slot_there = (0, 2, 1, 3)

    def device(y_there, z_there):
        return (lax.div(z_there, RUN) * half + rest, y_there * RUN + lax.rem(z_there, RUN))

    def y_of(apart):
        return lax.rem(y + apart, NY)

    def wait_for(ref, sem):
        pltpu.make_async_copy(ref, ref, sem).wait()

    def send(src, dst, send_sem, recv_sem, where):
        pltpu.make_async_remote_copy(
            src_ref=src, dst_ref=dst, send_sem=send_sem, recv_sem=recv_sem, device_id=where, device_id_type=MESH
        ).start()

    barrier = pltpu.get_barrier_semaphore()

    def greet(apart, carry):
        pl.semaphore_signal(barrier, inc=1, device_id=(dp, lax.rem(me + apart, SHARDS)), device_id_type=MESH)
        return carry

    lax.fori_loop(1, SHARDS, greet, 0)
    for slot in (1, 2, 3):

        @pl.when(lax.div(z_of[slot], RUN) != lax.div(z, RUN))
        def _(slot=slot):
            def greet_across(apart, carry):
                pl.semaphore_signal(
                    barrier, inc=1, device_id=device(y_of(apart), z_of[slot]), device_id_type=MESH
                )
                return carry

            lax.fori_loop(0, NY, greet_across, 0)

    def input_copies(q):
        span = pl.ds(pl.multiple_of(q * SUPER, 128), SUPER)
        return (
            pltpu.make_async_copy(gate_hbm.at[:, span], gate.at[:, span], load_sem.at[0, q]),
            pltpu.make_async_copy(up_hbm.at[:, span], up.at[:, span], load_sem.at[1, q]),
        )

    for q in range(supers):
        for copy in input_copies(q):
            copy.start()
    load_turn = pltpu.make_async_copy(turn_hbm, turn, load_sem.at[2, 0])
    load_scale = pltpu.make_async_copy(scale_hbm, scale, load_sem.at[2, 1])
    load_turn.start()
    load_scale.start()
    def code_copy(q):
        span = pl.ds(pl.multiple_of(q * CODE_ROWS, CODE_ROWS), CODE_ROWS)
        return pltpu.make_async_copy(codes_hbm.at[span, :], codes.at[span, :], code_sem.at[q])

    across = 1 + lax.rem(lax.div(z_lo + 1, 2) + 1, 2)
    for q in range(supers):
        code_copy(q).start()
    pl.semaphore_wait(barrier, SHARDS - 1 + NY * across)

    def send_hidden(q, carry):
        span = pl.ds(pl.multiple_of(q * SUPER, 128), SUPER)
        for copy in input_copies(q):
            copy.wait()

        def hidden_of(owner):
            its = pl.ds(pl.multiple_of(owner * piece, piece), piece)
            g = gate[its, span].astype(jnp.float32)
            value = g / (1.0 + jnp.exp(-g)) * up[its, span].astype(jnp.float32)
            return its, value.astype(jnp.bfloat16)

        mine = pl.ds(pl.multiple_of(me * piece, piece), piece)
        for apart in range(1, SHARDS):
            owner = lax.rem(me + apart, SHARDS)
            its, value = hidden_of(owner)
            hidden[its, span] = value
            send(
                hidden.at[its, span], gathered.at[mine, span], gather_send, gather_recv.at[q], (dp, owner)
            )
        its, value = hidden_of(me)
        gathered[its, span] = value
        return carry

    lax.fori_loop(0, supers, send_hidden, 0)
    load_turn.wait()
    load_scale.wait()

    def decode_levels(q):
        code_copy(q).wait()

        def decode(tile, inner):
            columns = pl.ds(pl.multiple_of(tile * 256, 256), 256)
            code_span = pl.ds(pl.multiple_of(q * CODE_ROWS, CODE_ROWS), CODE_ROWS)
            shifted = codes[code_span, columns].astype(jnp.int32) + 8388608
            for digit in range(6):
                value = jnp.bitwise_and(jnp.right_shift(shifted, 4 * digit), 15) - 8
                level_span = pl.ds(pl.multiple_of(q * SUPER + digit * CODE_ROWS, CODE_ROWS), CODE_ROWS)
                levels[level_span, columns] = value.astype(jnp.float32).astype(jnp.bfloat16)
            return inner

        lax.fori_loop(0, features // 256, decode, 0)

    def rotate(q, carry):
        span = pl.ds(pl.multiple_of(q * SUPER, 128), SUPER)
        pl.when(q < supers - 1)(lambda: decode_levels(q))
        wait_for(gathered.at[pl.ds(0, (SHARDS - 1) * piece), span], gather_recv.at[q])
        local = jnp.dot(gathered[:, span], turn[...], preferred_element_type=jnp.float32)
        terms = [local[piece * t : piece * (t + 1)] for t in range(SHARDS)]
        step = 1
        while step < SHARDS:
            after = list(terms)
            for t in range(SHARDS):
                if not t & step:
                    after[t] = terms[t] + terms[t + step]
                    after[t + step] = terms[t] - terms[t + step]
            terms, step = after, 2 * step
        scaling = 1.0 / math.sqrt(128 * SHARDS)
        for t in range(SHARDS):
            turned[piece * t : piece * (t + 1), span] = (terms[t] * scaling).astype(jnp.bfloat16)
        for slot in (3, 1, 2, 0):
            for apart in (2, 1, 3, 0):
                if slot == 0 and apart == 0:
                    continue
                shard = y_of(apart) * RUN + lax.rem(z_of[slot], RUN)
                row = (((NY - apart) % NY) * 4 + slot_there[slot]) * piece
                send(
                    turned.at[pl.ds(pl.multiple_of(shard * piece, piece), piece), span],
                    rot.at[pl.ds(row, piece), span],
                    scatter_send,
                    scatter_recv.at[q],
                    device(y_of(apart), z_of[slot]),
                )
        rot[0:piece, span] = turned[pl.ds(pl.multiple_of(me * piece, piece), piece), span]
        return carry

    lax.fori_loop(0, supers, rotate, 0)
    decode_levels(supers - 1)

    def wait_rotated(q):
        span = pl.ds(pl.multiple_of(q * SUPER, 128), SUPER)
        wait_for(rot.at[pl.ds(0, (SHARDS - 1) * piece), span], scatter_recv.at[q])
        return span

    def grow(q, carry):
        span = wait_rotated(q)
        first[...] += jnp.dot(
            rot[:, span], levels[span, 0 : FIRST * WIDTH], preferred_element_type=jnp.float32
        )
        return carry

    first[...] = jnp.zeros_like(first)
    lax.fori_loop(0, supers - 1, grow, 0)
    last_span = wait_rotated(supers - 1)

    def y_columns(c):
        t, kind = c
        return pl.ds(pl.multiple_of((t * PERIOD + kind) * WIDTH, 128), PATTERN[kind][0])

    def z_columns(c):
        t, kind = c
        return pl.ds(pl.multiple_of((t * PERIOD + kind) * WIDTH + PATTERN[kind][0], 128), PATTERN[kind][1])

    def far_columns(c):
        t, kind = c
        return pl.ds(pl.multiple_of(t * Z_SPAN + sum(z for _, z in PATTERN[:kind]), 128), PATTERN[kind][1])

    def index(c):
        return c[0] * PERIOD + c[1]

    shared_chunks = max(chunks - DIRECT, 0)

    def added(*values):
        total = values[0].astype(jnp.float32)
        for value in values[1:]:
            total = total + value.astype(jnp.float32)
        return total.astype(jnp.bfloat16)

    def rows_at(first, count):
        return pl.ds(first * piece, count * piece)

    y_above, y_below, y_across = (device(y_of(apart), z) for apart in (1, 3, 2))
    z_above, z_below, z_across = (device(y, z_of[slot]) for slot in (1, 2, 3))
    far_goes_down = z_lo < 2
    far_passes = lax.rem(z_lo, 3) == 0

    def multiply(c):
        columns = pl.ds(pl.multiple_of(index(c) * WIDTH, 128), WIDTH)
        start(c, jnp.dot(rot[...], levels[:, columns], preferred_element_type=jnp.float32))

    def start(c, product):
        columns = pl.ds(pl.multiple_of(index(c) * WIDTH, 128), WIDTH)
        product = (product * scale[:, columns]).astype(jnp.bfloat16)
        y_width = PATTERN[c[1]][0]
        part[:, y_columns(c)] = product[:, :y_width]
        for apart in range(NY):
            for slot in range(4):
                row = (apart * 4 + slot) * piece
                part[rows_at(slot * NY + apart, 1), z_columns(c)] = product[row : row + piece, y_width:]

        @pl.when(far_goes_down)
        def _():
            send(part.at[rows_at(12, 4), z_columns(c)], far_above.at[:, far_columns(c)], a_send, a_recv.at[3, index(c)], z_below)

        @pl.when(jnp.logical_not(far_goes_down))
        def _():
            send(part.at[rows_at(12, 4), z_columns(c)], far_below.at[:, far_columns(c)], a_send, a_recv.at[2, index(c)], z_above)

        send(part.at[rows_at(8, 2), y_columns(c)], from_below_a.at[:, y_columns(c)], a_send, a_recv.at[0, index(c)], y_above)
        send(part.at[rows_at(10, 2), y_columns(c)], from_above_a.at[:, y_columns(c)], a_send, a_recv.at[1, index(c)], y_below)

    def pass_on(c):
        wait_for(from_below_a.at[:, y_columns(c)], a_recv.at[0, index(c)])
        part[rows_at(4, 2), y_columns(c)] = added(part[rows_at(4, 2), y_columns(c)], from_below_a[:, y_columns(c)])
        send(part.at[rows_at(4, 4), y_columns(c)], from_below_b.at[:, y_columns(c)], b_send, b_recv.at[0, index(c)], y_above)
        wait_for(from_above_a.at[:, y_columns(c)], a_recv.at[1, index(c)])
        part[rows_at(14, 2), y_columns(c)] = added(part[rows_at(14, 2), y_columns(c)], from_above_a[:, y_columns(c)])
        send(part.at[rows_at(12, 4), y_columns(c)], from_above_b.at[:, y_columns(c)], b_send, b_recv.at[1, index(c)], y_below)

        @pl.when(far_passes)
        def _():
            wait_for(far_below.at[:, far_columns(c)], a_recv.at[2, index(c)])
            part[rows_at(4, 4), z_columns(c)] = added(part[rows_at(4, 4), z_columns(c)], far_below[:, far_columns(c)])
            wait_for(far_above.at[:, far_columns(c)], a_recv.at[3, index(c)])
            part[rows_at(8, 4), z_columns(c)] = added(part[rows_at(8, 4), z_columns(c)], far_above[:, far_columns(c)])

        send(part.at[rows_at(4, 4), z_columns(c)], from_below_b.at[:, z_columns(c)], b_send, b_recv.at[2, index(c)], z_above)
        send(part.at[rows_at(8, 4), z_columns(c)], from_above_b.at[:, z_columns(c)], b_send, b_recv.at[3, index(c)], z_below)

    def to_owners(c):
        def summed(columns, low):
            wait_for(from_below_b.at[:, columns], b_recv.at[low, index(c)])
            wait_for(from_above_b.at[:, columns], b_recv.at[low + 1, index(c)])
            part[rows_at(0, 4), columns] = added(
                part[rows_at(0, 4), columns], from_below_b[:, columns], from_above_b[:, columns]
            )

        def give(row, buffer, columns, sem, where):
            send(part.at[rows_at(row, 1), columns], buffer.at[:, columns], c_send, c_recv.at[sem, index(c)], where)

        shared = index(c) < shared_chunks
        summed(z_columns(c), 2)

        @pl.when(shared)
        def _():
            if c[1] % 2 == 0:
                give(2, from_below_c, z_columns(c), 2, y_above)
            else:
                give(2, from_above_c, z_columns(c), 2, y_below)

        @pl.when(jnp.logical_not(shared))
        def _():
            give_last(c, 2, 2, z_columns(c), 5, y_across, e_send)
            give_last(c, 1, 0, z_columns(c), 2, y_above, e_send)
            give_last(c, 3, 1, z_columns(c), 3, y_below, e_send)

        summed(y_columns(c), 0)

        @pl.when(shared)
        def _():
            pl.when(far_goes_down)(lambda: give(3, from_above_c, y_columns(c), 1, z_below))
            pl.when(jnp.logical_not(far_goes_down))(lambda: give(3, from_below_c, y_columns(c), 0, z_above))

        @pl.when(jnp.logical_not(shared))
        def _():
            give_last(c, 3, 2, y_columns(c), 4, z_across, e_send)
            give_last(c, 1, 0, y_columns(c), 0, z_above, e_send)
            give_last(c, 2, 1, y_columns(c), 1, z_below, e_send)

    def give_last(c, row, place, columns, sem, where, done):
        send(
            part.at[rows_at(row, 1), columns],
            from_next.at[rows_at(place, 1), columns],
            done,
            d_recv.at[sem, index(c)],
            where,
        )

    def last_hop(c):
        def add(row, buffer, columns, sem):
            wait_for(buffer.at[:, columns], c_recv.at[sem, index(c)])
            part[rows_at(row, 1), columns] = added(part[rows_at(row, 1), columns], buffer[:, columns])

        if c[1] % 2 == 0:
            add(1, from_below_c, z_columns(c), 2)
        else:
            add(3, from_above_c, z_columns(c), 2)
        give_last(c, 1, 0, z_columns(c), 2, y_above, d_send)
        give_last(c, 3, 1, z_columns(c), 3, y_below, d_send)

        @pl.when(far_passes)
        def _():
            add(1, from_below_c, y_columns(c), 0)
            add(2, from_above_c, y_columns(c), 1)

        give_last(c, 1, 0, y_columns(c), 0, z_above, d_send)
        give_last(c, 2, 1, y_columns(c), 1, z_below, d_send)

    def finish(c):
        def total(columns, sems):
            for place, sem in enumerate(sems):
                wait_for(from_next.at[rows_at(place, 1), columns], d_recv.at[sem, index(c)])
            out[:, columns] = added(
                part[rows_at(0, 1), columns], *(from_next[rows_at(place, 1), columns] for place in range(len(sems)))
            )

        @pl.when(index(c) < shared_chunks)
        def _():
            total(y_columns(c), (0, 1))
            total(z_columns(c), (2, 3))

        @pl.when(index(c) >= shared_chunks)
        def _():
            total(y_columns(c), (0, 1, 4))
            total(z_columns(c), (2, 3, 5))

        columns = pl.ds(pl.multiple_of(index(c) * WIDTH, 128), WIDTH)
        pltpu.make_async_copy(out.at[:, columns], out_hbm.at[:, columns], out_sem).start()

    def step(t, carry):
        for kind in range(PERIOD):
            for lag, work in zip((*LAGS, 0), (pass_on, to_owners, last_hop, finish, multiply)):
                chunk = (t + (kind - lag) // PERIOD, (kind - lag) % PERIOD)
                at = index(chunk)
                lowest = FIRST if lag == 0 else 0
                highest = shared_chunks if work is last_hop else chunks
                pl.when((at >= lowest) & (at < highest))(functools.partial(work, chunk))
        return carry

    for kind in range(FIRST):
        columns = slice(kind * WIDTH, (kind + 1) * WIDTH)
        product = jnp.dot(rot[:, last_span], levels[last_span, columns], preferred_element_type=jnp.float32)
        start((kind // PERIOD, kind % PERIOD), first[:, columns] + product)
    lax.fori_loop(0, (chunks + LAGS[-1] + PERIOD - 1) // PERIOD, step, 0)

    wait_for(out, out_sem)
    wait_for(gathered.at[pl.ds(0, (SHARDS - 1) * piece), :], gather_send)
    wait_for(rot.at[pl.ds(0, (SHARDS - 1) * piece), :], scatter_send)
    wait_for(part.at[rows_at(0, 4), :], a_send)
    wait_for(part.at[rows_at(0, 8), :], b_send)
    split = shared_chunks * WIDTH
    if split:
        wait_for(part.at[rows_at(0, 1), 0:split], c_send)
        wait_for(from_next.at[rows_at(0, 2), 0:split], d_send)
    if split < features:
        wait_for(from_next.at[:, split:features], e_send)


def body(gate_inputs, up_inputs, down_codes, column_scale, half):
    rows, hidden_width = gate_inputs.shape
    code_rows, features = down_codes.shape
    chunks = features // WIDTH
    supers = hidden_width // SUPER
    piece, block = rows // SHARDS, rows // NY
    outside = pl.BlockSpec(memory_space=pl.ANY)
    b16 = jnp.bfloat16
    return pl.pallas_call(
        functools.partial(kernel, half),
        out_shape=jax.ShapeDtypeStruct((piece, features), b16),
        in_specs=[outside] * 5,
        out_specs=outside,
        scratch_shapes=[
            pltpu.VMEM((piece, features), b16),
            pltpu.VMEM((1, features), jnp.float32),
            pltpu.VMEM((SUPER, SUPER), b16),
            pltpu.VMEM((rows, hidden_width), b16),
            pltpu.VMEM((rows, hidden_width), b16),
            pltpu.VMEM((code_rows, features), jnp.float32),
            pltpu.VMEM((rows, hidden_width), b16),
            pltpu.VMEM((rows, hidden_width), b16),
            pltpu.VMEM((rows, hidden_width), b16),
            pltpu.VMEM((rows, hidden_width), b16),
            pltpu.VMEM((hidden_width, features), b16),
            pltpu.VMEM((rows, FIRST * WIDTH), jnp.float32),
            pltpu.VMEM((rows, features), b16),
            pltpu.VMEM((block // 2, features), b16),
            pltpu.VMEM((block // 2, features), b16),
            pltpu.VMEM((block, chunks // PERIOD * Z_SPAN), b16),
            pltpu.VMEM((block, chunks // PERIOD * Z_SPAN), b16),
            pltpu.VMEM((block, features), b16),
            pltpu.VMEM((block, features), b16),
            pltpu.VMEM((piece, features), b16),
            pltpu.VMEM((piece, features), b16),
            pltpu.VMEM((3 * piece, features), b16),
            pltpu.SemaphoreType.DMA,
            pltpu.SemaphoreType.DMA((3, supers)),
            pltpu.SemaphoreType.DMA((supers,)),
            pltpu.SemaphoreType.DMA,
            pltpu.SemaphoreType.DMA((supers,)),
            pltpu.SemaphoreType.DMA,
            pltpu.SemaphoreType.DMA((supers,)),
            pltpu.SemaphoreType.DMA,
            pltpu.SemaphoreType.DMA((4, chunks)),
            pltpu.SemaphoreType.DMA,
            pltpu.SemaphoreType.DMA((4, chunks)),
            pltpu.SemaphoreType.DMA,
            pltpu.SemaphoreType.DMA((3, chunks)),
            pltpu.SemaphoreType.DMA,
            pltpu.SemaphoreType.DMA,
            pltpu.SemaphoreType.DMA((6, chunks)),
        ],
        compiler_params=pltpu.CompilerParams(
            collective_id=0, has_side_effects=True, vmem_limit_bytes=60 * 1024 * 1024
        ),
    )(gate_inputs, up_inputs, down_codes, column_scale.reshape(1, features), jnp.asarray(turn_matrix()))


def solution(mesh):
    return jax.shard_map(
        functools.partial(body, half=mesh.shape["dp"] // 2),
        mesh=mesh,
        in_specs=(P("dp", "tensor"), P("dp", "tensor"), P("tensor", None), P()),
        out_specs=P(("dp", "tensor"), None),
        check_vma=False,
    )
```

```python
import functools
import math

import jax
import jax.numpy as jnp
import ml_dtypes
import numpy as np
from jax import lax
from jax.experimental import pallas as pl
from jax.experimental.pallas import tpu as pltpu
from jax.sharding import PartitionSpec as P

MESH = pl.DeviceIdType.MESH
NY, NZ, RUN = 4, 8, 4
SHARDS = NY * RUN
SUPER = 384
CODE_ROWS = SUPER // 6
PATTERN = ((384, 128), (256, 256))
PERIOD = len(PATTERN)
WIDTH = sum(PATTERN[0])
DIRECT = 6
FIRST = 4
Z_SPAN = sum(z_width for _, z_width in PATTERN)
LAGS = 5, 9, 13, 17


def sylvester(extent):
    indices = np.arange(extent)
    common = indices[:, None] & indices[None, :]
    parity = np.zeros((extent, extent), np.int64)
    for offset in range(extent.bit_length() - 1):
        parity += (common >> offset) & 1
    return 1 - 2 * (parity % 2)


def turn_matrix():
    blocks = np.kron(np.eye(SUPER // 128), sylvester(128))
    order = np.arange(SUPER).reshape(CODE_ROWS, 6).T.reshape(-1)
    return blocks[:, order].astype(ml_dtypes.bfloat16)


def kernel(
    half,
    gate_hbm,
    up_hbm,
    codes_hbm,
    scale_hbm,
    turn_hbm,
    out_hbm,
    out,
    scale,
    turn,
    gate,
    up,
    codes,
    hidden,
    gathered,
    turned,
    rot,
    levels,
    first,
    part,
    from_below_a,
    from_above_a,
    far_below,
    far_above,
    from_below_b,
    from_above_b,
    from_below_c,
    from_above_c,
    from_next,
    out_sem,
    load_sem,
    code_sem,
    gather_send,
    gather_recv,
    scatter_send,
    scatter_recv,
    a_send,
    a_recv,
    b_send,
    b_recv,
    c_send,
    c_recv,
    d_send,
    e_send,
    d_recv,
):
    rows, hidden_width = gate.shape
    features = levels.shape[1]
    supers = hidden_width // SUPER
    piece = rows // SHARDS
    chunks = features // WIDTH
    dp = lax.axis_index("dp")
    me = lax.axis_index("tensor")
    rest = lax.rem(dp, half)
    y = lax.div(me, RUN)
    z_lo = lax.rem(me, RUN)
    z = lax.div(dp, half) * RUN + z_lo
    z_far = lax.rem(z + 6 - 4 * lax.div(z_lo, 2), NZ)
    z_of = (z, lax.rem(z + 1, NZ), lax.rem(z + NZ - 1, NZ), z_far)
    slot_there = (0, 2, 1, 3)

    def device(y_there, z_there):
        return (lax.div(z_there, RUN) * half + rest, y_there * RUN + lax.rem(z_there, RUN))

    def y_of(apart):
        return lax.rem(y + apart, NY)

    def wait_for(ref, sem):
        pltpu.make_async_copy(ref, ref, sem).wait()

    def send(src, dst, send_sem, recv_sem, where):
        pltpu.make_async_remote_copy(
            src_ref=src, dst_ref=dst, send_sem=send_sem, recv_sem=recv_sem, device_id=where, device_id_type=MESH
        ).start()

    barrier = pltpu.get_barrier_semaphore()

    def greet(apart, carry):
        pl.semaphore_signal(barrier, inc=1, device_id=(dp, lax.rem(me + apart, SHARDS)), device_id_type=MESH)
        return carry

    lax.fori_loop(1, SHARDS, greet, 0)
    for slot in (1, 2, 3):

        @pl.when(lax.div(z_of[slot], RUN) != lax.div(z, RUN))
        def _(slot=slot):
            def greet_across(apart, carry):
                pl.semaphore_signal(
                    barrier, inc=1, device_id=device(y_of(apart), z_of[slot]), device_id_type=MESH
                )
                return carry

            lax.fori_loop(0, NY, greet_across, 0)

    def input_copies(q):
        span = pl.ds(pl.multiple_of(q * SUPER, 128), SUPER)
        return (
            pltpu.make_async_copy(gate_hbm.at[:, span], gate.at[:, span], load_sem.at[0, q]),
            pltpu.make_async_copy(up_hbm.at[:, span], up.at[:, span], load_sem.at[1, q]),
        )

    for q in range(supers):
        for copy in input_copies(q):
            copy.start()
    load_turn = pltpu.make_async_copy(turn_hbm, turn, load_sem.at[2, 0])
    load_scale = pltpu.make_async_copy(scale_hbm, scale, load_sem.at[2, 1])
    load_turn.start()
    load_scale.start()
    def code_copy(q):
        span = pl.ds(pl.multiple_of(q * CODE_ROWS, CODE_ROWS), CODE_ROWS)
        return pltpu.make_async_copy(codes_hbm.at[span, :], codes.at[span, :], code_sem.at[q])

    across = 1 + lax.rem(lax.div(z_lo + 1, 2) + 1, 2)
    for q in range(supers):
        code_copy(q).start()
    pl.semaphore_wait(barrier, SHARDS - 1 + NY * across)

    def send_hidden(q, carry):
        span = pl.ds(pl.multiple_of(q * SUPER, 128), SUPER)
        for copy in input_copies(q):
            copy.wait()

        def hidden_of(owner):
            its = pl.ds(pl.multiple_of(owner * piece, piece), piece)
            g = gate[its, span].astype(jnp.float32)
            value = g / (1.0 + jnp.exp(-g)) * up[its, span].astype(jnp.float32)
            return its, value.astype(jnp.bfloat16)

        mine = pl.ds(pl.multiple_of(me * piece, piece), piece)
        for apart in range(1, SHARDS):
            owner = lax.rem(me + apart, SHARDS)
            its, value = hidden_of(owner)
            hidden[its, span] = value
            send(
                hidden.at[its, span], gathered.at[mine, span], gather_send, gather_recv.at[q], (dp, owner)
            )
        its, value = hidden_of(me)
        gathered[its, span] = value
        return carry

    lax.fori_loop(0, supers, send_hidden, 0)
    load_turn.wait()
    load_scale.wait()

    def decode_levels(q):
        code_copy(q).wait()

        def decode(tile, inner):
            columns = pl.ds(pl.multiple_of(tile * 256, 256), 256)
            code_span = pl.ds(pl.multiple_of(q * CODE_ROWS, CODE_ROWS), CODE_ROWS)
            shifted = codes[code_span, columns].astype(jnp.int32) + 8388608
            for digit in range(6):
                value = jnp.bitwise_and(jnp.right_shift(shifted, 4 * digit), 15) - 8
                level_span = pl.ds(pl.multiple_of(q * SUPER + digit * CODE_ROWS, CODE_ROWS), CODE_ROWS)
                levels[level_span, columns] = value.astype(jnp.float32).astype(jnp.bfloat16)
            return inner

        lax.fori_loop(0, features // 256, decode, 0)

    def rotate(q, carry):
        span = pl.ds(pl.multiple_of(q * SUPER, 128), SUPER)
        pl.when(q < supers - 1)(lambda: decode_levels(q))
        wait_for(gathered.at[pl.ds(0, (SHARDS - 1) * piece), span], gather_recv.at[q])
        local = jnp.dot(gathered[:, span], turn[...], preferred_element_type=jnp.float32)
        terms = [local[piece * t : piece * (t + 1)] for t in range(SHARDS)]
        step = 1
        while step < SHARDS:
            after = list(terms)
            for t in range(SHARDS):
                if not t & step:
                    after[t] = terms[t] + terms[t + step]
                    after[t + step] = terms[t] - terms[t + step]
            terms, step = after, 2 * step
        scaling = 1.0 / math.sqrt(128 * SHARDS)
        for t in range(SHARDS):
            turned[piece * t : piece * (t + 1), span] = (terms[t] * scaling).astype(jnp.bfloat16)
        for slot in (3, 1, 2, 0):
            for apart in (2, 1, 3, 0):
                if slot == 0 and apart == 0:
                    continue
                shard = y_of(apart) * RUN + lax.rem(z_of[slot], RUN)
                row = (((NY - apart) % NY) * 4 + slot_there[slot]) * piece
                send(
                    turned.at[pl.ds(pl.multiple_of(shard * piece, piece), piece), span],
                    rot.at[pl.ds(row, piece), span],
                    scatter_send,
                    scatter_recv.at[q],
                    device(y_of(apart), z_of[slot]),
                )
        rot[0:piece, span] = turned[pl.ds(pl.multiple_of(me * piece, piece), piece), span]
        return carry

    lax.fori_loop(0, supers, rotate, 0)
    decode_levels(supers - 1)

    def wait_rotated(q):
        span = pl.ds(pl.multiple_of(q * SUPER, 128), SUPER)
        wait_for(rot.at[pl.ds(0, (SHARDS - 1) * piece), span], scatter_recv.at[q])
        return span

    def grow(q, carry):
        span = wait_rotated(q)
        first[...] += jnp.dot(
            rot[:, span], levels[span, 0 : FIRST * WIDTH], preferred_element_type=jnp.float32
        )
        return carry

    first[...] = jnp.zeros_like(first)
    lax.fori_loop(0, supers - 1, grow, 0)
    last_span = wait_rotated(supers - 1)

    def y_columns(c):
        t, kind = c
        return pl.ds(pl.multiple_of((t * PERIOD + kind) * WIDTH, 128), PATTERN[kind][0])

    def z_columns(c):
        t, kind = c
        return pl.ds(pl.multiple_of((t * PERIOD + kind) * WIDTH + PATTERN[kind][0], 128), PATTERN[kind][1])

    def far_columns(c):
        t, kind = c
        return pl.ds(pl.multiple_of(t * Z_SPAN + sum(z for _, z in PATTERN[:kind]), 128), PATTERN[kind][1])

    def index(c):
        return c[0] * PERIOD + c[1]

    shared_chunks = max(chunks - DIRECT, 0)

    def added(*values):
        total = values[0].astype(jnp.float32)
        for value in values[1:]:
            total = total + value.astype(jnp.float32)
        return total.astype(jnp.bfloat16)

    def rows_at(first, count):
        return pl.ds(first * piece, count * piece)

    y_above, y_below, y_across = (device(y_of(apart), z) for apart in (1, 3, 2))
    z_above, z_below, z_across = (device(y, z_of[slot]) for slot in (1, 2, 3))
    far_goes_down = z_lo < 2
    far_passes = lax.rem(z_lo, 3) == 0

    def multiply(c):
        columns = pl.ds(pl.multiple_of(index(c) * WIDTH, 128), WIDTH)
        start(c, jnp.dot(rot[...], levels[:, columns], preferred_element_type=jnp.float32))

    def start(c, product):
        columns = pl.ds(pl.multiple_of(index(c) * WIDTH, 128), WIDTH)
        product = (product * scale[:, columns]).astype(jnp.bfloat16)
        y_width = PATTERN[c[1]][0]
        part[:, y_columns(c)] = product[:, :y_width]
        for apart in range(NY):
            for slot in range(4):
                row = (apart * 4 + slot) * piece
                part[rows_at(slot * NY + apart, 1), z_columns(c)] = product[row : row + piece, y_width:]

        send(part.at[rows_at(8, 2), y_columns(c)], from_below_a.at[:, y_columns(c)], a_send, a_recv.at[0, index(c)], y_above)
        send(part.at[rows_at(10, 2), y_columns(c)], from_above_a.at[:, y_columns(c)], a_send, a_recv.at[1, index(c)], y_below)

        @pl.when(far_goes_down)
        def _():
            send(part.at[rows_at(12, 4), z_columns(c)], far_above.at[:, far_columns(c)], a_send, a_recv.at[3, index(c)], z_below)

        @pl.when(jnp.logical_not(far_goes_down))
        def _():
            send(part.at[rows_at(12, 4), z_columns(c)], far_below.at[:, far_columns(c)], a_send, a_recv.at[2, index(c)], z_above)

    def pass_on(c):
        wait_for(from_below_a.at[:, y_columns(c)], a_recv.at[0, index(c)])
        part[rows_at(4, 2), y_columns(c)] = added(part[rows_at(4, 2), y_columns(c)], from_below_a[:, y_columns(c)])
        send(part.at[rows_at(4, 4), y_columns(c)], from_below_b.at[:, y_columns(c)], b_send, b_recv.at[0, index(c)], y_above)
        wait_for(from_above_a.at[:, y_columns(c)], a_recv.at[1, index(c)])
        part[rows_at(14, 2), y_columns(c)] = added(part[rows_at(14, 2), y_columns(c)], from_above_a[:, y_columns(c)])
        send(part.at[rows_at(12, 4), y_columns(c)], from_above_b.at[:, y_columns(c)], b_send, b_recv.at[1, index(c)], y_below)

        @pl.when(far_passes)
        def _():
            wait_for(far_below.at[:, far_columns(c)], a_recv.at[2, index(c)])
            part[rows_at(4, 4), z_columns(c)] = added(part[rows_at(4, 4), z_columns(c)], far_below[:, far_columns(c)])
            wait_for(far_above.at[:, far_columns(c)], a_recv.at[3, index(c)])
            part[rows_at(8, 4), z_columns(c)] = added(part[rows_at(8, 4), z_columns(c)], far_above[:, far_columns(c)])

        send(part.at[rows_at(4, 4), z_columns(c)], from_below_b.at[:, z_columns(c)], b_send, b_recv.at[2, index(c)], z_above)
        send(part.at[rows_at(8, 4), z_columns(c)], from_above_b.at[:, z_columns(c)], b_send, b_recv.at[3, index(c)], z_below)

    def to_owners(c):
        def summed(columns, low):
            wait_for(from_below_b.at[:, columns], b_recv.at[low, index(c)])
            wait_for(from_above_b.at[:, columns], b_recv.at[low + 1, index(c)])
            part[rows_at(0, 4), columns] = added(
                part[rows_at(0, 4), columns], from_below_b[:, columns], from_above_b[:, columns]
            )

        def give(row, buffer, columns, sem, where):
            send(part.at[rows_at(row, 1), columns], buffer.at[:, columns], c_send, c_recv.at[sem, index(c)], where)

        shared = index(c) < shared_chunks
        summed(z_columns(c), 2)

        @pl.when(shared)
        def _():
            if c[1] % 2 == 0:
                give(2, from_below_c, z_columns(c), 2, y_above)
            else:
                give(2, from_above_c, z_columns(c), 2, y_below)

        @pl.when(jnp.logical_not(shared))
        def _():
            give_last(c, 2, 2, z_columns(c), 5, y_across, e_send)
            give_last(c, 1, 0, z_columns(c), 2, y_above, e_send)
            give_last(c, 3, 1, z_columns(c), 3, y_below, e_send)

        summed(y_columns(c), 0)

        @pl.when(shared)
        def _():
            pl.when(far_goes_down)(lambda: give(3, from_above_c, y_columns(c), 1, z_below))
            pl.when(jnp.logical_not(far_goes_down))(lambda: give(3, from_below_c, y_columns(c), 0, z_above))

        @pl.when(jnp.logical_not(shared))
        def _():
            give_last(c, 3, 2, y_columns(c), 4, z_across, e_send)
            give_last(c, 1, 0, y_columns(c), 0, z_above, e_send)
            give_last(c, 2, 1, y_columns(c), 1, z_below, e_send)

    def give_last(c, row, place, columns, sem, where, done):
        send(
            part.at[rows_at(row, 1), columns],
            from_next.at[rows_at(place, 1), columns],
            done,
            d_recv.at[sem, index(c)],
            where,
        )

    def last_hop(c):
        def add(row, buffer, columns, sem):
            wait_for(buffer.at[:, columns], c_recv.at[sem, index(c)])
            part[rows_at(row, 1), columns] = added(part[rows_at(row, 1), columns], buffer[:, columns])

        if c[1] % 2 == 0:
            add(1, from_below_c, z_columns(c), 2)
        else:
            add(3, from_above_c, z_columns(c), 2)
        give_last(c, 1, 0, z_columns(c), 2, y_above, d_send)
        give_last(c, 3, 1, z_columns(c), 3, y_below, d_send)

        @pl.when(far_passes)
        def _():
            add(1, from_below_c, y_columns(c), 0)
            add(2, from_above_c, y_columns(c), 1)

        give_last(c, 1, 0, y_columns(c), 0, z_above, d_send)
        give_last(c, 2, 1, y_columns(c), 1, z_below, d_send)

    def finish(c):
        def total(columns, sems):
            for place, sem in enumerate(sems):
                wait_for(from_next.at[rows_at(place, 1), columns], d_recv.at[sem, index(c)])
            out[:, columns] = added(
                part[rows_at(0, 1), columns], *(from_next[rows_at(place, 1), columns] for place in range(len(sems)))
            )

        @pl.when(index(c) < shared_chunks)
        def _():
            total(y_columns(c), (0, 1))
            total(z_columns(c), (2, 3))

        @pl.when(index(c) >= shared_chunks)
        def _():
            total(y_columns(c), (0, 1, 4))
            total(z_columns(c), (2, 3, 5))

        columns = pl.ds(pl.multiple_of(index(c) * WIDTH, 128), WIDTH)
        pltpu.make_async_copy(out.at[:, columns], out_hbm.at[:, columns], out_sem).start()

    def step(t, carry):
        for kind in range(PERIOD):
            for lag, work in zip((*LAGS, 0), (pass_on, to_owners, last_hop, finish, multiply)):
                chunk = (t + (kind - lag) // PERIOD, (kind - lag) % PERIOD)
                at = index(chunk)
                lowest = FIRST if lag == 0 else 0
                highest = shared_chunks if work is last_hop else chunks
                pl.when((at >= lowest) & (at < highest))(functools.partial(work, chunk))
        return carry

    for kind in range(FIRST):
        columns = slice(kind * WIDTH, (kind + 1) * WIDTH)
        product = jnp.dot(rot[:, last_span], levels[last_span, columns], preferred_element_type=jnp.float32)
        start((kind // PERIOD, kind % PERIOD), first[:, columns] + product)
    lax.fori_loop(0, (chunks + LAGS[-1] + PERIOD - 1) // PERIOD, step, 0)

    wait_for(out, out_sem)
    wait_for(gathered.at[pl.ds(0, (SHARDS - 1) * piece), :], gather_send)
    wait_for(rot.at[pl.ds(0, (SHARDS - 1) * piece), :], scatter_send)
    wait_for(part.at[rows_at(0, 4), :], a_send)
    wait_for(part.at[rows_at(0, 8), :], b_send)
    split = shared_chunks * WIDTH
    if split:
        wait_for(part.at[rows_at(0, 1), 0:split], c_send)
        wait_for(from_next.at[rows_at(0, 2), 0:split], d_send)
    if split < features:
        wait_for(from_next.at[:, split:features], e_send)


def body(gate_inputs, up_inputs, down_codes, column_scale, half):
    rows, hidden_width = gate_inputs.shape
    code_rows, features = down_codes.shape
    chunks = features // WIDTH
    supers = hidden_width // SUPER
    piece, block = rows // SHARDS, rows // NY
    outside = pl.BlockSpec(memory_space=pl.ANY)
    b16 = jnp.bfloat16
    return pl.pallas_call(
        functools.partial(kernel, half),
        out_shape=jax.ShapeDtypeStruct((piece, features), b16),
        in_specs=[outside] * 5,
        out_specs=outside,
        scratch_shapes=[
            pltpu.VMEM((piece, features), b16),
            pltpu.VMEM((1, features), jnp.float32),
            pltpu.VMEM((SUPER, SUPER), b16),
            pltpu.VMEM((rows, hidden_width), b16),
            pltpu.VMEM((rows, hidden_width), b16),
            pltpu.VMEM((code_rows, features), jnp.float32),
            pltpu.VMEM((rows, hidden_width), b16),
            pltpu.VMEM((rows, hidden_width), b16),
            pltpu.VMEM((rows, hidden_width), b16),
            pltpu.VMEM((rows, hidden_width), b16),
            pltpu.VMEM((hidden_width, features), b16),
            pltpu.VMEM((rows, FIRST * WIDTH), jnp.float32),
            pltpu.VMEM((rows, features), b16),
            pltpu.VMEM((block // 2, features), b16),
            pltpu.VMEM((block // 2, features), b16),
            pltpu.VMEM((block, chunks // PERIOD * Z_SPAN), b16),
            pltpu.VMEM((block, chunks // PERIOD * Z_SPAN), b16),
            pltpu.VMEM((block, features), b16),
            pltpu.VMEM((block, features), b16),
            pltpu.VMEM((piece, features), b16),
            pltpu.VMEM((piece, features), b16),
            pltpu.VMEM((3 * piece, features), b16),
            pltpu.SemaphoreType.DMA,
            pltpu.SemaphoreType.DMA((3, supers)),
            pltpu.SemaphoreType.DMA((supers,)),
            pltpu.SemaphoreType.DMA,
            pltpu.SemaphoreType.DMA((supers,)),
            pltpu.SemaphoreType.DMA,
            pltpu.SemaphoreType.DMA((supers,)),
            pltpu.SemaphoreType.DMA,
            pltpu.SemaphoreType.DMA((4, chunks)),
            pltpu.SemaphoreType.DMA,
            pltpu.SemaphoreType.DMA((4, chunks)),
            pltpu.SemaphoreType.DMA,
            pltpu.SemaphoreType.DMA((3, chunks)),
            pltpu.SemaphoreType.DMA,
            pltpu.SemaphoreType.DMA,
            pltpu.SemaphoreType.DMA((6, chunks)),
        ],
        compiler_params=pltpu.CompilerParams(
            collective_id=0, has_side_effects=True, vmem_limit_bytes=60 * 1024 * 1024
        ),
    )(gate_inputs, up_inputs, down_codes, column_scale.reshape(1, features), jnp.asarray(turn_matrix()))


def solution(mesh):
    return jax.shard_map(
        functools.partial(body, half=mesh.shape["dp"] // 2),
        mesh=mesh,
        in_specs=(P("dp", "tensor"), P("dp", "tensor"), P("tensor", None), P()),
        out_specs=P(("dp", "tensor"), None),
        check_vma=False,
    )
```
